32 devices in a mesh: row: 4 (over x, core), col: 8 (over z, y).
Axes of the slice: x: 2, y: 2, z: 4, core: 2. Of those that a mesh axis runs over, the one named last changes fastest.
Arguments:
- observed: bfloat16 [512, 8, 128, 128], P(('row', 'col')), may hold values from -6 to 6
- sku_ids: int32 [512], P(('row', 'col')), may hold values from 0 to 15
- store_ids: int32 [512, 8], P(('row', 'col')), may hold values from 0 to 39
- live_slot_counts: int32 [4, 8, 4], P('row', 'col'), may hold values from 0 to 4, as said below
- sku_factors: float32 [65536, 256], P(('row', 'col')), may hold values from -1.5 to 1.5
- store_factors: float32 [20480, 256], P(('row', 'col')), may hold values from -1.5 to 1.5
Outputs:
- new_sku_factors: float32 [65536, 256], P(('row', 'col'))
- new_store_factors: float32 [20480, 256], P(('row', 'col'))
The draws below stay inside these ranges and needn't reach their ends.
Inputs may be any that keep to these rules, and one draw needn't show every extreme that they name: `live_slot_counts`: in every column index some owner row's slots are full from every device of that column.
All inputs are finite; a program needn't handle non-finite values.
Results may differ from the reference program's by a relative error of at most 0.023.
Values may be sent and summed in bfloat16 or wider, within the bound.
No kernel may reach another device: no remote copies, remote signals or barrier semaphores. Data moves between devices by JAX's collectives and lax.ppermute only.
A program may use at most 192 MiB of HBM per device.

```python
import jax
import jax.numpy as jnp
from jax import lax

R = 256
BS = 128
K = 8
SLOT_CAPACITY = 4
UB_DEV = 16
VB_DEV = 5
SLOT_ROWS = 512
VG = 40
NSKU = 65536
NSTORE = 20480
N_ROW = 4
N_COL = 8


def draw_live_slot_counts(key, part):
    first_key = jax.random.fold_in(key, 11)
    second_key = jax.random.fold_in(key, 12)
    busy_key = jax.random.fold_in(key, 13)
    full_key = jax.random.fold_in(key, 14)
    first = jax.random.randint(first_key, (N_ROW, N_COL, N_ROW), 0, SLOT_CAPACITY + 1)
    second = jax.random.randint(second_key, (N_ROW, N_COL, N_ROW), 0, SLOT_CAPACITY + 1)
    busy = jax.random.randint(busy_key, (1, N_COL, N_ROW), 0, 2)
    counts = jnp.where(busy == 1, jnp.maximum(first, second), jnp.minimum(first, second))
    full_owner = jax.random.randint(full_key, (1, N_COL, 1), 0, N_ROW)
    owner_index = lax.broadcasted_iota(jnp.int32, (N_ROW, N_COL, N_ROW), 2)
    return jnp.where(owner_index == full_owner, SLOT_CAPACITY, counts).astype(jnp.int32)


def set_ends(result, key, low, top_value):
    spot = [jax.random.randint(jax.random.fold_in(key, axis), (), 0, length) for axis, length in enumerate(result.shape)]
    main_axis = result.shape.index(max(result.shape))
    neighbour = spot[:main_axis] + [(spot[main_axis] + 1) % result.shape[main_axis]] + spot[main_axis + 1:]
    return result.at[tuple(spot)].set(low).at[tuple(neighbour)].set(top_value)


def shard_levels(key, shape, shards, low, high):
    level = 1.0
    for dim, parts in shards:
        steps = jax.random.uniform(jax.random.fold_in(jax.random.fold_in(key, 6), dim), (parts,), jnp.float32, low / len(shards), high / len(shards))
        level = level * jnp.repeat(jnp.exp(steps), shape[dim] // parts).reshape((-1,) + (1,) * (len(shape) - 1 - dim))
    return level


def noise(key, dims, width, limit, cuts=(), kind=jnp.bfloat16):
    array = width * jax.random.normal(key, dims, jnp.float32)
    if cuts:
        array = array * shard_levels(key, dims, cuts, -0.22, 0.18)
    return jnp.clip(array, -limit, limit).astype(kind)


def setup_inputs(seed: int = 0) -> dict:
    seeds = jax.random.split(jax.random.key(seed), 7)
    observed = noise(seeds[0], (SLOT_ROWS, K, BS, BS), 1.0, 6.0, ((0, 32),))
    sku_ids = set_ends(jax.random.randint(seeds[1], (SLOT_ROWS,), 0, UB_DEV), jax.random.fold_in(seeds[1], 1), 0, UB_DEV - 1).astype(jnp.int32)
    store_ids = set_ends(jax.random.randint(seeds[2], (SLOT_ROWS, K), 0, VG), jax.random.fold_in(seeds[2], 1), 0, VG - 1).astype(jnp.int32)
    live_slot_counts = draw_live_slot_counts(jax.random.fold_in(seeds[6], 71), 0)
    sku_factors = noise(seeds[4], (NSKU, R), 0.25, 1.5, ((0, 32),), jnp.float32)
    store_factors = noise(seeds[5], (NSTORE, R), 0.25, 1.5, ((0, 32),), jnp.float32)
    return {"observed": observed, "sku_ids": sku_ids, "store_ids": store_ids, "live_slot_counts": live_slot_counts, "sku_factors": sku_factors, "store_factors": store_factors}


learn_rate = 0.01
weight_decay = 0.05


def reference(observed, sku_ids, store_ids, live_slot_counts, sku_factors, store_factors):
    total_live_slots = SLOT_CAPACITY * N_ROW
    all_slots = total_live_slots * N_ROW * N_COL
    position = jnp.arange(all_slots, dtype=jnp.int32)
    device = position // total_live_slots
    within_owner = position % total_live_slots
    owner_row = within_owner // SLOT_CAPACITY
    row_of = device // N_COL
    col_of = device % N_COL
    counts_flat = live_slot_counts.reshape(N_ROW * N_COL, N_ROW)
    slot_limits = counts_flat[device, owner_row]
    slot_alive_mask = (within_owner % SLOT_CAPACITY < slot_limits).astype(jnp.float32)
    product_global_index = ((owner_row * N_COL + col_of) * UB_DEV + sku_ids).astype(jnp.int32)
    shop_global_index = (row_of[:, None] * (VB_DEV * N_COL) + store_ids).astype(jnp.int32)
    sku_blocks = sku_factors.reshape(-1, BS, R)
    store_blocks = store_factors.reshape(-1, BS, R)
    sku_low = sku_blocks.astype(jnp.bfloat16)
    store_low = store_blocks.astype(jnp.bfloat16)
    groups = all_slots // 8

    def split_into_groups(array_in):
        return array_in.reshape((groups, 8) + array_in.shape[1:])

    input_arrays = (split_into_groups(product_global_index), split_into_groups(shop_global_index), split_into_groups(observed), split_into_groups(slot_alive_mask))

    def misfit_of(sku_pick, store_pick, measured, store_table):
        selected_rows = sku_low[sku_pick].astype(jnp.float32)
        selected_cols = store_table[store_pick].astype(jnp.float32)
        predicted = jnp.einsum("sar,skbr->skab", selected_rows, selected_cols, precision=lax.Precision.HIGHEST)
        misfit = (predicted - measured.astype(jnp.float32)).astype(jnp.bfloat16)
        misfit = lax.optimization_barrier(misfit).astype(jnp.float32)
        return misfit, selected_rows, selected_cols

    def first_pass(running, inputs_now):
        sku_pick, store_pick, measured, alive = inputs_now
        misfit, selected_rows, selected_cols = misfit_of(sku_pick, store_pick, measured, store_low)
        partial_value = jnp.einsum("skab,sar->skbr", misfit, selected_rows, precision=lax.Precision.HIGHEST)
        partial_value = partial_value * alive[:, None, None, None]
        running = running.at[store_pick.reshape(-1)].add(partial_value.reshape(-1, BS, R))
        return running, None

    store_grad, _ = lax.scan(first_pass, jnp.zeros(store_blocks.shape, jnp.float32), input_arrays)
    new_store = store_blocks - learn_rate * (store_grad + weight_decay * store_blocks)
    new_store_low = new_store.astype(jnp.bfloat16)

    def second_pass(running, inputs_now):
        sku_pick, store_pick, measured, alive = inputs_now
        misfit, selected_rows, selected_cols = misfit_of(sku_pick, store_pick, measured, new_store_low)
        partial_value = jnp.einsum("skab,skbr->sar", misfit, selected_cols, precision=lax.Precision.HIGHEST)
        partial_value = partial_value * alive[:, None, None]
        running = running.at[sku_pick].add(partial_value)
        return running, None

    sku_grad, _ = lax.scan(second_pass, jnp.zeros(sku_blocks.shape, jnp.float32), input_arrays)
    new_sku = sku_blocks - learn_rate * (sku_grad + weight_decay * sku_blocks)
    return new_sku.reshape(sku_factors.shape), new_store.reshape(store_factors.shape)
```

```python
import functools

import jax
import jax.numpy as jnp
from jax import lax
from jax.experimental import pallas as pl
from jax.experimental.pallas import tpu as pltpu
from jax.sharding import PartitionSpec as P

learn_rate = 0.01
weight_decay = 0.05
line_len = 4

VMEM = pltpu.VMEM
SMEM = pltpu.SMEM


def ring_place(col, col_count):
    width = max(col_count // line_len, 1)
    depth = col_count // width
    across, along = col % width, col // width
    return across * depth + jnp.where(across % 2 == 0, along, depth - 1 - along)


def ring_steps(col_count):
    width = max(col_count // line_len, 1)
    depth = col_count // width
    order = []
    for place in range(col_count):
        across, along = divmod(place, depth)
        along = along if across % 2 == 0 else depth - 1 - along
        order.append(along * width + across)
    ahead = [(order[p], order[(p + 1) % col_count]) for p in range(col_count)]
    back = [(b, a) for a, b in ahead]
    return ahead, back


def spec(space):
    return pl.BlockSpec(memory_space=space)


def gather_ring(rows, col_count):
    ahead, back = ring_steps(col_count)
    half = rows.shape[0] // 2
    far = col_count // 2
    parts = [rows[:half], rows[half:]]
    from_behind, from_front = list(parts), list(parts)
    pieces = {(0, 0): parts[0], (0, 1): parts[1]}
    for step in range(1, far + 1):
        for h in (0, 1):
            if step < far or h == 0:
                from_behind[h] = lax.ppermute(from_behind[h], "col", ahead)
                pieces[(col_count - step, h)] = from_behind[h]
            if step < far or h == 1:
                from_front[h] = lax.ppermute(from_front[h], "col", back)
                pieces[(step, h)] = from_front[h]
    return pieces


def scatter_ring(pieces, col_count):
    ahead, back = ring_steps(col_count)
    far = col_count // 2
    sums = []
    to_front = [pieces[(far, 0)], pieces[(far - 1, 1)]]
    to_back = [pieces[(col_count - far + 1, 0)], pieces[(far, 1)]]
    for step in range(far, 0, -1):
        for h in (0, 1):
            if step < far or h == 0:
                moved = lax.ppermute(to_front[h], "col", ahead)
                if step > 1:
                    moved = (
                        moved.astype(jnp.float32) + pieces[(step - 1, h)].astype(jnp.float32)
                    ).astype(jnp.bfloat16)
                to_front[h] = moved
            if step < far or h == 1:
                moved = lax.ppermute(to_back[h], "col", back)
                if step > 1:
                    moved = (
                        moved.astype(jnp.float32)
                        + pieces[(col_count - step + 1, h)].astype(jnp.float32)
                    ).astype(jnp.bfloat16)
                to_back[h] = moved
    for h in (0, 1):
        sums.append(
            pieces[(0, h)].astype(jnp.float32)
            + to_front[h].astype(jnp.float32)
            + to_back[h].astype(jnp.float32)
        )
    return jnp.concatenate(sums, axis=0)


def pick_kernel(row_count, per_owner, row_ref, *refs):
    ids = refs[:row_count]
    table = refs[row_count]
    outs = refs[row_count + 1 : 2 * row_count + 1]
    held, sems = refs[2 * row_count + 1 :]
    row = row_ref[0]

    def copy_of(k, i):
        block = ids[k][row * per_owner + i]
        n = k * per_owner + i
        return pltpu.make_async_copy(table.at[block], held.at[n], sems.at[n])

    for k in range(row_count):
        for i in range(per_owner):
            copy_of(k, i).start()
    for k in range(row_count):
        for i in range(per_owner):
            copy_of(k, i).wait()
            outs[k][i] = held[k * per_owner + i].astype(jnp.bfloat16)


def pick(row, ids, table, per_owner):
    row_count = len(ids)
    block = table.shape[1:]
    return pl.pallas_call(
        functools.partial(pick_kernel, row_count, per_owner),
        out_shape=[jax.ShapeDtypeStruct((per_owner,) + block, jnp.bfloat16)] * row_count,
        in_specs=[spec(SMEM)] * (row_count + 1) + [spec(pl.ANY)],
        out_specs=[spec(VMEM)] * row_count,
        scratch_shapes=[
            VMEM((row_count * per_owner,) + block, jnp.float32),
            pltpu.SemaphoreType.DMA((row_count * per_owner,)),
        ],
        compiler_params=pltpu.CompilerParams(vmem_limit_bytes=48 * 1024 * 1024),
    )(row, *ids, table)


def load_table(table, names, refs, rows):
    half = rows // 2
    for (offset, h), ref in zip(names, refs):
        table[pl.ds(offset * rows + h * half, half), :] = ref[...]


def first_kernel(cfg, row_ref, live_ref, ids_ref, observed, *refs):
    row_count, per_owner, kinds, block, rows, names = cfg
    skus = refs[:row_count]
    pieces = refs[row_count : row_count + len(names)]
    outs = refs[row_count + len(names) : row_count + 2 * len(names)]
    table, grad = refs[row_count + 2 * len(names) :]
    row = row_ref[0]
    load_table(table, names, pieces, rows)
    grad[...] = jnp.zeros_like(grad)
    for k in range(row_count):
        owner = row ^ k

        @pl.loop(0, live_ref[owner])
        def _(i):
            slot = owner * per_owner + i
            sku = skus[k][i]
            terms = []
            for n in range(kinds):
                at = pl.multiple_of(ids_ref[slot * kinds + n] * block, block)
                store = table[pl.ds(at, block), :]
                predicted = lax.dot_general(
                    sku, store, (((1,), (1,)), ((), ())), preferred_element_type=jnp.float32
                )
                misfit = (predicted - observed[slot, n].astype(jnp.float32)).astype(jnp.bfloat16)
                terms.append(
                    lax.dot_general(
                        misfit, sku, (((0,), (0,)), ((), ())), preferred_element_type=jnp.float32
                    )
                )
            for n in range(kinds):
                at = pl.multiple_of(ids_ref[slot * kinds + n] * block, block)
                grad[pl.ds(at, block), :] += terms[n]

    half = rows // 2
    for (offset, h), out in zip(names, outs):
        out[...] = grad[pl.ds(offset * rows + h * half, half), :].astype(jnp.bfloat16)


def second_kernel(cfg, row_ref, live_ref, ids_ref, observed, *refs):
    row_count, per_owner, kinds, block, rows, names = cfg
    skus = refs[:row_count]
    pieces = refs[row_count : row_count + len(names)]
    outs = refs[row_count + len(names) : 2 * row_count + len(names)]
    (table,) = refs[2 * row_count + len(names) :]
    row = row_ref[0]
    load_table(table, names, pieces, rows)
    for k in range(row_count):
        owner = row ^ k
        outs[k][...] = jnp.zeros_like(outs[k])

        @pl.loop(0, live_ref[owner])
        def _(i):
            slot = owner * per_owner + i
            sku = skus[k][i]
            total = None
            for n in range(kinds):
                at = pl.multiple_of(ids_ref[slot * kinds + n] * block, block)
                store = table[pl.ds(at, block), :]
                predicted = lax.dot_general(
                    sku, store, (((1,), (1,)), ((), ())), preferred_element_type=jnp.float32
                )
                misfit = (predicted - observed[slot, n].astype(jnp.float32)).astype(jnp.bfloat16)
                term = jnp.dot(misfit, store, preferred_element_type=jnp.float32)
                total = term if total is None else total + term
            outs[k][i] = total.astype(jnp.bfloat16)


def run_pass(kernel, second, row, live, ids, observed, skus, pieces, cfg):
    row_count, per_owner, kinds, block, rows, names = cfg
    rank = skus[0].shape[2]
    columns = max(offset for offset, _ in names) + 1
    if second:
        outs = [jax.ShapeDtypeStruct(skus[0].shape, jnp.bfloat16)] * row_count
        scratch = [VMEM((columns * rows, rank), jnp.bfloat16)]
    else:
        outs = [jax.ShapeDtypeStruct((rows // 2, rank), jnp.bfloat16)] * len(names)
        scratch = [
            VMEM((columns * rows, rank), jnp.bfloat16),
            VMEM((columns * rows, rank), jnp.float32),
        ]
    return pl.pallas_call(
        functools.partial(kernel, cfg),
        out_shape=outs,
        in_specs=[spec(SMEM)] * 3 + [spec(VMEM)] * (1 + row_count + len(names)),
        out_specs=[spec(VMEM)] * len(outs),
        scratch_shapes=scratch,
        compiler_params=pltpu.CompilerParams(vmem_limit_bytes=56 * 1024 * 1024),
    )(row, live, ids, observed, *skus, *[pieces[name] for name in names])


def finish_kernel(row_count, per_owner, row_ref, *refs):
    ids = refs[:row_count]
    sku = refs[row_count]
    terms = refs[row_count + 1 : 2 * row_count + 1]
    out = refs[2 * row_count + 1]
    (grad,) = refs[2 * row_count + 2 :]
    row = row_ref[0]
    grad[...] = jnp.zeros_like(grad)
    for k in range(row_count):
        for i in range(per_owner):
            block = ids[k][row * per_owner + i]
            grad[block] += terms[k][i].astype(jnp.float32)
    out[...] = sku[...] - learn_rate * (grad[...] + weight_decay * sku[...])


def finish(row, ids, sku, terms, per_owner):
    row_count = len(ids)
    return pl.pallas_call(
        functools.partial(finish_kernel, row_count, per_owner),
        out_shape=jax.ShapeDtypeStruct(sku.shape, jnp.float32),
        in_specs=[spec(SMEM)] * (row_count + 1) + [spec(VMEM)] * (1 + row_count),
        out_specs=spec(VMEM),
        scratch_shapes=[VMEM(sku.shape, jnp.float32)],
        compiler_params=pltpu.CompilerParams(vmem_limit_bytes=48 * 1024 * 1024),
    )(row, *ids, sku, *terms)


def local(observed, sku_ids, store_ids, live_slot_counts, sku_factors, store_factors):
    row_count = lax.axis_size("row")
    col_count = lax.axis_size("col")
    per_owner = observed.shape[0] // row_count
    kinds, block = observed.shape[1:3]
    rank = sku_factors.shape[1]
    rows = store_factors.shape[0]
    store_blocks = rows // block
    row = lax.axis_index("row")
    row_vec = row.reshape(1).astype(jnp.int32)
    live = live_slot_counts.reshape(row_count)
    sku = sku_factors.reshape(-1, block, rank)

    swaps = [[(r, r ^ k) for r in range(row_count)] for k in range(row_count)]
    asked = [sku_ids] + [lax.ppermute(sku_ids, "row", swaps[k]) for k in range(1, row_count)]

    place = ring_place(lax.axis_index("col"), col_count)
    owner_place = ring_place(store_ids // store_blocks, col_count)
    near_ids = ((owner_place - place) % col_count) * store_blocks + store_ids % store_blocks
    near_ids = near_ids.reshape(-1)

    names = [(d, h) for d in range(col_count) for h in (0, 1)]
    cfg = (row_count, per_owner, kinds, block, rows, names)

    pieces = gather_ring(store_factors.astype(jnp.bfloat16), col_count)
    picked = pick(row_vec, asked, sku, per_owner)
    skus = [picked[0]] + [
        lax.ppermute(picked[k], "row", swaps[k]) for k in range(1, row_count)
    ]
    grads = run_pass(first_kernel, False, row_vec, live, near_ids, observed, skus, pieces, cfg)
    own_grad = scatter_ring(dict(zip(names, grads)), col_count)
    new_store = store_factors - learn_rate * (own_grad + weight_decay * store_factors)
    new_pieces = gather_ring(new_store.astype(jnp.bfloat16), col_count)
    terms = run_pass(second_kernel, True, row_vec, live, near_ids, observed, skus, new_pieces, cfg)
    arrived = [terms[0]] + [
        lax.ppermute(terms[k], "row", swaps[k]) for k in range(1, row_count)
    ]
    new_sku = finish(row_vec, asked, sku, arrived, per_owner)
    return new_sku.reshape(sku_factors.shape), new_store


def solution(mesh):
    placed = (
        P(("row", "col"), None, None, None),
        P(("row", "col")),
        P(("row", "col"), None),
        P("row", "col", None),
        P(("row", "col"), None),
        P(("row", "col"), None),
    )
    return jax.shard_map(
        local,
        mesh=mesh,
        in_specs=placed,
        out_specs=(P(("row", "col"), None), P(("row", "col"), None)),
        check_vma=False,
    )
```

```python
import functools

import jax
import jax.numpy as jnp
from jax import lax
from jax.experimental import pallas as pl
from jax.experimental.pallas import tpu as pltpu
from jax.sharding import PartitionSpec as P

learn_rate = 0.01
weight_decay = 0.05
line_len = 4
batch = 8

VMEM = pltpu.VMEM
SMEM = pltpu.SMEM
NT = (((1,), (1,)), ((), ()))


def spec(space):
    return pl.BlockSpec(memory_space=space)


def near(array):
    return pltpu.with_memory_space_constraint(array, VMEM)


def away(array):
    return pltpu.with_memory_space_constraint(array, pltpu.HBM)


def params(mib):
    return pltpu.CompilerParams(vmem_limit_bytes=mib * 1024 * 1024)


def cost(pairs, block, rank):
    return pl.CostEstimate(
        flops=pairs * 4 * block * block * rank,
        bytes_accessed=pairs * 256 * 1024,
        transcendentals=0,
    )


def ring_place(col, col_count):
    width = max(col_count // line_len, 1)
    depth = col_count // width
    across, along = col % width, col // width
    return across * depth + jnp.where(across % 2 == 0, along, depth - 1 - along)


def ring_steps(col_count):
    width = max(col_count // line_len, 1)
    depth = col_count // width
    order = []
    for place in range(col_count):
        across, along = divmod(place, depth)
        along = along if across % 2 == 0 else depth - 1 - along
        order.append(along * width + across)
    ahead = [(order[p], order[(p + 1) % col_count]) for p in range(col_count)]
    back = [(b, a) for a, b in ahead]
    return ahead, back


class Plan:
    def __init__(self, col_count, rows, block):
        self.count = col_count
        self.far = col_count // 2
        self.rows, self.block = rows, block
        self.blocks = rows // block
        first = (self.blocks + 1) // 2 * block
        self.halves = [(0, first), (first, rows)]
        self.order = [0]
        for m in range(1, self.far):
            self.order += [m, col_count - m]
        self.order.append(self.far)
        self.groups = [self.order[:3], self.order[3:-3], self.order[-3:]]
        self.starts = [self.order.index(g[0]) * self.blocks for g in self.groups]

    def arrival(self, offset):
        back = self.count - offset
        return jnp.where(
            offset == 0,
            0,
            jnp.where(
                offset == self.far,
                self.count - 1,
                jnp.where(offset < self.far, 2 * offset - 1, 2 * back),
            ),
        )

    def cuts(self, offset):
        return self.halves if offset == self.far else [(0, self.rows)]


def after(value, mark):
    return jnp.where(mark[0, :1] < jnp.inf, value, jnp.zeros_like(value))


def gather_ring(low, plan, mark_last=lambda pieces: None):
    steps = ring_steps(plan.count)
    moved = [low, low]
    pieces = {0: [low]}
    for step in range(1, plan.far):
        for way in (0, 1):
            moved[way] = lax.ppermute(moved[way], "col", steps[way])
            pieces[step if way else plan.count - step] = [moved[way]]
    mark = mark_last(pieces)
    parts = [moved[way][a:b] for way, (a, b) in enumerate(plan.halves)]
    if mark is not None:
        parts = [after(part, mark) for part in parts]
    pieces[plan.far] = [lax.ppermute(parts[way], "col", steps[way]) for way in (0, 1)]
    return pieces


def add_up(moved, piece):
    return (moved.astype(jnp.float32) + piece.astype(jnp.float32)).astype(jnp.bfloat16)


def scatter_ring(pieces, plan):
    steps = ring_steps(plan.count)
    first = plan.halves[0][1]
    moved = [lax.ppermute(pieces[plan.far][way], "col", steps[way]) for way in (0, 1)]
    for step in range(plan.far - 1, 0, -1):
        for way in (0, 1):
            (value,) = pieces[plan.count - step if way else step]
            if step == plan.far - 1:
                parts = [value[:first], value[first:]]
                parts[way] = add_up(moved[way], parts[way])
                value = jnp.concatenate(parts, axis=0)
            else:
                value = add_up(moved[way], value)
            moved[way] = lax.ppermute(value, "col", steps[way])
    return (
        pieces[0][0].astype(jnp.float32)
        + moved[0].astype(jnp.float32)
        + moved[1].astype(jnp.float32)
    )


def pick_kernel(row_count, per_owner, row_ref, *refs):
    ids = refs[:row_count]
    table, *outs = refs[row_count:-2]
    held, sems = refs[-2:]
    row = row_ref[0]

    def block_of(k, i):
        n = k * per_owner + i
        block = ids[k][row * per_owner + i]
        return pltpu.make_async_copy(table.at[block], held.at[n], sems.at[n])

    order = [(k, i) for k in reversed(range(row_count)) for i in range(per_owner)]
    for k, i in order:
        block_of(k, i).start()
    for k, i in order:
        block_of(k, i).wait()
        out = outs[k] if k < 2 else outs[1 + k // 2]
        at = i if k < 2 else k % 2 * per_owner + i
        out[at] = held[k * per_owner + i].astype(jnp.bfloat16)


def pick(row, ids, table, per_owner):
    row_count = len(ids)
    block, rank = table.shape[1:]
    heights = [per_owner] * 2 + [2 * per_owner] * (row_count // 2 - 1)
    shapes = [VMEM((height, block, rank), jnp.bfloat16) for height in heights]
    asked = row_count * per_owner
    return pl.pallas_call(
        functools.partial(pick_kernel, row_count, per_owner),
        out_shape=shapes,
        in_specs=[spec(SMEM)] * (row_count + 1) + [spec(pltpu.HBM)],
        out_specs=[spec(VMEM)] * len(shapes),
        scratch_shapes=[
            VMEM((asked, block, rank), jnp.float32),
            pltpu.SemaphoreType.DMA((asked,)),
        ],
        compiler_params=params(8),
    )(row, *ids, away(table))


def join_kernel(per_owner, first, *refs):
    out = refs[-1]
    out[0:per_owner] = first[...]
    for x in range(1, out.shape[0] // per_owner):
        out[x * per_owner : (x + 1) * per_owner] = refs[x - 1][per_owner:]


def join(first, moved, per_owner, marks):
    shape = ((1 + len(moved)) * per_owner,) + first.shape[1:]
    inputs = [first, *moved, *marks]
    return pl.pallas_call(
        functools.partial(join_kernel, per_owner),
        out_shape=VMEM(shape, first.dtype),
        in_specs=[spec(VMEM)] * len(inputs),
        out_specs=spec(VMEM),
        compiler_params=params(1),
    )(*map(near, inputs))


def list_kernel(cfg, row_ref, live_ref, ids_ref, observed, *refs):
    row_count, per_owner, kinds, starts, room = cfg
    pairs_ref, counts_ref, held, sem = refs[-4:]
    copy = pltpu.make_async_copy(observed, held, sem)
    copy.start()
    row = row_ref[0]
    for g in range(len(starts)):
        counts_ref[g] = 0
    for owner in range(row_count):

        @pl.loop(0, live_ref[owner])
        def _(i):
            slot = owner * per_owner + i
            sku_at = (row ^ owner) * per_owner + i
            for n in range(kinds):
                at = ids_ref[slot, n]
                group = jnp.int32(0)
                for start in starts[1:]:
                    group += (at >= start).astype(jnp.int32)
                filled = counts_ref[group]
                pairs_ref[group * room + filled] = at + n * 256 + sku_at * 4096 + slot * 1048576
                counts_ref[group] = filled + 1

    for g, start in enumerate(starts):
        for q in range(batch - 1):
            blank = start + row_count * per_owner * 4096
            pairs_ref[g * room + counts_ref[g] + q] = jnp.int32(blank)
    copy.wait()


def list_pairs(row, live, ids, observed, plan, row_count, per_owner, kinds, marks):
    room = row_count * per_owner * kinds + batch
    groups = len(plan.groups)
    return pl.pallas_call(
        functools.partial(list_kernel, (row_count, per_owner, kinds, plan.starts, room)),
        out_shape=[
            jax.ShapeDtypeStruct((groups * room,), jnp.int32),
            jax.ShapeDtypeStruct((groups,), jnp.int32),
            VMEM(observed.shape, observed.dtype),
        ],
        in_specs=[spec(SMEM)] * 3 + [spec(pltpu.HBM)] + [spec(VMEM)] * len(marks),
        out_specs=[spec(SMEM)] * 2 + [spec(VMEM)],
        scratch_shapes=[pltpu.SemaphoreType.DMA],
        compiler_params=params(1),
    )(row, live, ids, away(observed), *map(near, marks))


def load_skus(held, refs, starts):
    count = refs[0].shape[0]
    for k, (ref, start) in enumerate(zip(refs, starts)):
        held[pl.ds(k * count, count)] = ref[start : start + count]
    held[len(refs) * count] = jnp.zeros_like(held[0])


def load_table(table, refs):
    at = 0
    for ref in refs:
        table[pl.ds(at, ref.shape[0]), :] = ref[...]
        at += ref.shape[0]


def for_pairs(pairs_ref, counts_ref, room, groups, base, block, body):
    for g in groups:

        @pl.loop(0, pl.cdiv(counts_ref[g], batch))
        def _(b):
            entries = []
            for q in range(batch):
                e = pairs_ref[g * room + b * batch + q]
                at = pl.multiple_of(((e & 255) - base) * block, block)
                entries.append((at, (e >> 8) & 15, (e >> 12) & 255, e >> 20))
            body(entries)


def first_kernel(cfg, pairs_ref, counts_ref, observed, *refs):
    sku_starts, piece_count, out_count, room, groups, base, block = cfg
    sku_count = len(sku_starts)
    skus = refs[:sku_count]
    pieces = refs[sku_count : sku_count + piece_count]
    outs = refs[-3 - out_count : -3]
    held, table, grad = refs[-3:]
    load_skus(held, skus, sku_starts)
    load_table(table, pieces)
    grad[...] = jnp.zeros_like(grad)

    def body(entries):
        terms = []
        for at, n, sku_at, slot in entries:
            sku = held[sku_at]
            predicted = lax.dot_general(
                table[pl.ds(at, block), :], sku, NT, preferred_element_type=jnp.float32
            )
            misfit = predicted - observed[slot, n].T.astype(jnp.float32)
            terms.append(
                jnp.dot(misfit.astype(jnp.bfloat16), sku, preferred_element_type=jnp.float32)
            )
        for (at, _, _, _), term in zip(entries, terms):
            grad[pl.ds(at, block), :] += term

    for_pairs(pairs_ref, counts_ref, room, groups, base, block, body)
    at = 0
    for out in outs:
        out[...] = grad[pl.ds(at, out.shape[0]), :].astype(jnp.bfloat16)
        at += out.shape[0]


def first_pass(pairs, counts, observed, skus, pieces, plan, groups, marks):
    offsets = [d for g in groups for d in plan.groups[g]]
    given = [piece for d in offsets for piece in pieces[d]]
    cuts = [plan.cuts(d) for d in offsets]
    heights = [b - a for spans in cuts for a, b in spans]
    skus, sku_starts = zip(*skus)
    block, rank = plan.block, skus[0].shape[2]
    room = pairs.shape[0] // len(plan.groups)
    slots = len(skus) * skus[0].shape[0]
    cfg = (sku_starts, len(given), len(heights), room, groups, plan.starts[groups[0]], block)
    table = (len(offsets) * plan.rows, rank)
    inputs = [observed, *skus, *given, *marks]
    out = pl.pallas_call(
        functools.partial(first_kernel, cfg),
        out_shape=[VMEM((height, rank), jnp.bfloat16) for height in heights],
        in_specs=[spec(SMEM)] * 2 + [spec(VMEM)] * len(inputs),
        out_specs=[spec(VMEM)] * len(heights),
        scratch_shapes=[
            VMEM((slots + 1, block, rank), jnp.bfloat16),
            VMEM(table, jnp.bfloat16),
            VMEM(table, jnp.float32),
        ],
        compiler_params=params(24),
        cost_estimate=cost(len(offsets) * room // plan.count, block, rank),
    )(pairs, counts, *map(near, inputs))
    out = list(out)
    return {d: [out.pop(0) for _ in spans] for d, spans in zip(offsets, cuts)}


def second_kernel(cfg, row_ref, live_ref, ids_ref, observed, *refs):
    ks, sku_starts, per_owner, kinds, block = cfg
    skus, pieces = refs[: len(ks)], refs[len(ks) : -1 - len(ks)]
    outs, table = refs[-1 - len(ks) : -1], refs[-1]
    load_table(table, pieces)
    row = row_ref[0]
    for k, sku_ref, start, out in zip(ks, skus, sku_starts, outs):
        out[...] = jnp.zeros_like(out)
        owner = row ^ k

        @pl.loop(0, live_ref[owner])
        def _(i):
            slot = owner * per_owner + i
            stores, measured = [], []
            for n in range(kinds):
                at = pl.multiple_of(ids_ref[slot, n] * block, block)
                stores.append(table[pl.ds(at, block), :])
                measured.append(observed[slot, n])
            store = jnp.concatenate(stores, axis=0)
            predicted = lax.dot_general(
                sku_ref[start + i], store, NT, preferred_element_type=jnp.float32
            )
            misfit = predicted - jnp.concatenate(measured, axis=1).astype(jnp.float32)
            out[i] = jnp.dot(
                misfit.astype(jnp.bfloat16), store, preferred_element_type=jnp.float32
            ).astype(jnp.bfloat16)


def second_pass(ks, row, live, ids, observed, skus, pieces, plan, per_owner):
    kept, sku_starts = zip(*[skus[k] for k in ks])
    kinds, block, rank = observed.shape[1], plan.block, kept[0].shape[2]
    shape = (per_owner, block, rank)
    inputs = [observed, *kept, *[piece for d in plan.order for piece in pieces[d]]]
    return pl.pallas_call(
        functools.partial(second_kernel, (ks, sku_starts, per_owner, kinds, block)),
        out_shape=[VMEM(shape, jnp.bfloat16)] * len(ks),
        in_specs=[spec(SMEM)] * 3 + [spec(VMEM)] * len(inputs),
        out_specs=[spec(VMEM)] * len(ks),
        scratch_shapes=[VMEM((plan.count * plan.rows, rank), jnp.bfloat16)],
        compiler_params=params(16),
        cost_estimate=cost(len(ks) * per_owner * kinds, block, rank),
    )(row, live, ids, *map(near, inputs))


def take_terms(held, ids, terms, row, per_owner):
    blocks = []
    for block_ids, term in zip(ids, terms):
        for i in range(per_owner):
            block = block_ids[row * per_owner + i]
            held[block] -= learn_rate * term[i].astype(jnp.float32)
            blocks.append(block)
    return blocks


def copy_out(held, out, blocks, sems):
    copies = [
        pltpu.make_async_copy(held.at[block], out.at[block], sems.at[n])
        for n, block in enumerate(blocks)
    ]
    for copy in copies:
        copy.start()
    for copy in copies:
        copy.wait()


def base_kernel(count, per_owner, row_ref, *refs):
    ids, sku, terms = refs[:count], refs[count], refs[count + 1 : -3]
    held, out, sems = refs[-3:]
    held[...] = sku[...] * (1.0 - learn_rate * weight_decay)
    take_terms(held, ids, terms, row_ref[0], per_owner)
    copy_out(held, out, range(sku.shape[0]), sems)


def base_step(row, ids, sku, terms, per_owner):
    return pl.pallas_call(
        functools.partial(base_kernel, len(ids), per_owner),
        out_shape=[VMEM(sku.shape, jnp.float32), pltpu.HBM(sku.shape, jnp.float32)],
        in_specs=[spec(SMEM)] * (len(ids) + 1) + [spec(VMEM)] * (1 + len(ids)),
        out_specs=[spec(VMEM), spec(pltpu.HBM)],
        scratch_shapes=[pltpu.SemaphoreType.DMA((sku.shape[0],))],
        compiler_params=params(8),
    )(row, *ids, sku, *map(near, terms))


def finish_kernel(count, per_owner, row_ref, *refs):
    ids, sku, terms = refs[:count], refs[count], refs[count + 1 : 2 * count + 1]
    out, held, sems = refs[-3:]
    for block_ids in ids:
        for i in range(per_owner):
            block = block_ids[row_ref[0] * per_owner + i]
            held[block] = sku[block]
    blocks = take_terms(held, ids, terms, row_ref[0], per_owner)
    copy_out(held, out, blocks, sems)


def finish_step(row, ids, held, out, terms, per_owner):
    return pl.pallas_call(
        functools.partial(finish_kernel, len(ids), per_owner),
        out_shape=pltpu.HBM(out.shape, jnp.float32),
        in_specs=[spec(SMEM)] * (len(ids) + 1)
        + [spec(VMEM)] * (1 + len(ids))
        + [spec(pltpu.HBM)],
        out_specs=spec(pltpu.HBM),
        scratch_shapes=[
            VMEM(out.shape, jnp.float32),
            pltpu.SemaphoreType.DMA((len(ids) * per_owner,)),
        ],
        input_output_aliases={2 + 2 * len(ids): 0},
        compiler_params=params(4),
    )(row, *ids, near(held), *map(near, terms), away(out))


def local(observed, sku_ids, store_ids, live_slot_counts, sku_factors, store_factors):
    row_count = lax.axis_size("row")
    per_owner = observed.shape[0] // row_count
    kinds, block = observed.shape[1:3]
    rank = sku_factors.shape[1]
    plan = Plan(lax.axis_size("col"), store_factors.shape[0], block)
    row_vec = lax.axis_index("row").reshape(1).astype(jnp.int32)
    live = live_slot_counts.reshape(row_count)
    sku = sku_factors.reshape(-1, block, rank)

    swaps = [[(r, r ^ k) for r in range(row_count)] for k in range(row_count)]
    asked = [sku_ids] + [lax.ppermute(sku_ids, "row", swaps[k]) for k in range(1, row_count)]
    picked = pick(row_vec, asked, sku, per_owner)
    moved = [
        lax.ppermute(picked[1 + x], "row", swaps[2 * x]) for x in range(1, row_count // 2)
    ]

    place = ring_place(lax.axis_index("col"), plan.count)
    owner_place = ring_place(store_ids // plan.blocks, plan.count)
    arrival = plan.arrival((owner_place - place) % plan.count)
    ids = arrival * plan.blocks + store_ids % plan.blocks
    made = []

    def prepare(pieces):
        early = pieces[1] + pieces[plan.count - 1]
        made.extend(
            list_pairs(
                row_vec, live, ids, observed, plan, row_count, per_owner, kinds, early
            )
        )
        late = pieces[plan.far - 2] + pieces[plan.far + 2] + [made[2]]
        made.append(
            lax.ppermute(join(picked[1], moved, per_owner, late), "row", swaps[1])
        )
        return made[3][0]

    pieces = gather_ring(store_factors.astype(jnp.bfloat16), plan, prepare)
    pairs, counts, observed, passed = made
    skus = [(picked[0], 0), (passed, 0)]
    for x, both in enumerate(moved, 1):
        skus += [(both, 0), (passed, x * per_owner)]

    grads, marks = {}, []
    for group in (0, 2, 1):
        if plan.groups[group]:
            some = first_pass(pairs, counts, observed, skus, pieces, plan, [group], marks)
            grads.update(some)
            marks = some[plan.groups[group][0]][:1]
    own_grad = scatter_ring(grads, plan)
    new_store = store_factors - learn_rate * (own_grad + weight_decay * store_factors)
    new_pieces = gather_ring(new_store.astype(jnp.bfloat16), plan)

    terms = [None] * row_count
    for ks in (list(range(2, row_count)), [1, 0]):
        out = second_pass(ks, row_vec, live, ids, observed, skus, new_pieces, plan, per_owner)
        for k, term in zip(ks, out):
            terms[k] = lax.ppermute(term, "row", swaps[k]) if k else term
    held, new_sku = base_step(row_vec, asked[:2], sku, terms[:2], per_owner)
    new_sku = finish_step(row_vec, asked[2:], held, new_sku, terms[2:], per_owner)
    return new_sku.reshape(sku_factors.shape), new_store


def solution(mesh):
    placed = (
        P(("row", "col"), None, None, None),
        P(("row", "col")),
        P(("row", "col"), None),
        P("row", "col", None),
        P(("row", "col"), None),
        P(("row", "col"), None),
    )
    return jax.shard_map(
        local,
        mesh=mesh,
        in_specs=placed,
        out_specs=(P(("row", "col"), None), P(("row", "col"), None)),
        check_vma=False,
    )
```

```python
import functools

import jax
import jax.numpy as jnp
from jax import lax
from jax.experimental import pallas as pl
from jax.experimental.pallas import tpu as pltpu
from jax.sharding import PartitionSpec as P

learn_rate = 0.01
weight_decay = 0.05
line_len = 4
batch = 8

VMEM = pltpu.VMEM
SMEM = pltpu.SMEM
NT = (((1,), (1,)), ((), ()))


def spec(space):
    return pl.BlockSpec(memory_space=space)


def near(array):
    return pltpu.with_memory_space_constraint(array, VMEM)


def away(array):
    return pltpu.with_memory_space_constraint(array, pltpu.HBM)


def params(mib):
    return pltpu.CompilerParams(vmem_limit_bytes=mib * 1024 * 1024)


def cost(pairs, block, rank):
    return pl.CostEstimate(
        flops=pairs * 4 * block * block * rank,
        bytes_accessed=pairs * 256 * 1024,
        transcendentals=0,
    )


def ring_place(col, col_count):
    width = max(col_count // line_len, 1)
    depth = col_count // width
    across, along = col % width, col // width
    return across * depth + jnp.where(across % 2 == 0, along, depth - 1 - along)


def ring_steps(col_count):
    width = max(col_count // line_len, 1)
    depth = col_count // width
    order = []
    for place in range(col_count):
        across, along = divmod(place, depth)
        along = along if across % 2 == 0 else depth - 1 - along
        order.append(along * width + across)
    ahead = [(order[p], order[(p + 1) % col_count]) for p in range(col_count)]
    back = [(b, a) for a, b in ahead]
    return ahead, back


class Plan:
    def __init__(self, col_count, rows, block):
        self.count = col_count
        self.far = col_count // 2
        self.rows, self.block = rows, block
        self.blocks = rows // block
        first = (self.blocks + 1) // 2 * block
        self.halves = [(0, first), (first, rows)]
        self.order = [0]
        for m in range(1, self.far):
            self.order += [m, col_count - m]
        self.order.append(self.far)
        self.groups = [self.order[:3], self.order[3:-3], self.order[-3:-1], self.order[-1:]]
        self.starts = [self.order.index(g[0]) * self.blocks for g in self.groups]

    def arrival(self, offset):
        back = self.count - offset
        return jnp.where(
            offset == 0,
            0,
            jnp.where(
                offset == self.far,
                self.count - 1,
                jnp.where(offset < self.far, 2 * offset - 1, 2 * back),
            ),
        )

    def cuts(self, offset):
        return self.halves if offset == self.far else [(0, self.rows)]


def after(value, mark):
    return jnp.where(mark[:1] < jnp.inf, value, jnp.zeros_like(value))


def gather_ring(low, plan, marks=None, arrived=None):
    steps = ring_steps(plan.count)
    moved = [low, low]
    pieces = {0: [low]}
    for step in range(1, plan.far + 1):
        if step == plan.far:
            moved = [moved[way][a:b] for way, (a, b) in enumerate(plan.halves)]
        if marks and step in marks:
            moved = [after(value, marks[step]) for value in moved]
        moved = [lax.ppermute(moved[way], "col", steps[way]) for way in (0, 1)]
        if step == plan.far:
            pieces[step] = moved
        else:
            pieces[plan.count - step] = moved[:1]
            pieces[step] = moved[1:]
        if arrived:
            arrived(step, pieces)
    return pieces


def add_up(moved, piece):
    return (moved.astype(jnp.float32) + piece.astype(jnp.float32)).astype(jnp.bfloat16)


def scatter_ring(pieces, plan):
    steps = ring_steps(plan.count)
    first = plan.halves[0][1]
    moved = [lax.ppermute(pieces[plan.far][way], "col", steps[way]) for way in (0, 1)]
    for step in range(plan.far - 1, 0, -1):
        for way in (0, 1):
            (value,) = pieces[plan.count - step if way else step]
            if step == plan.far - 1:
                parts = [value[:first], value[first:]]
                parts[way] = add_up(moved[way], parts[way])
                value = jnp.concatenate(parts, axis=0)
            else:
                value = add_up(moved[way], value)
            moved[way] = lax.ppermute(value, "col", steps[way])
    return (
        pieces[0][0].astype(jnp.float32)
        + moved[0].astype(jnp.float32)
        + moved[1].astype(jnp.float32)
    )


def pick_kernel(row_count, per_owner, row_ref, *refs):
    ids = refs[:row_count]
    table, *outs = refs[row_count:-2]
    held, sems = refs[-2:]
    row = row_ref[0]

    def block_of(k, i):
        n = k * per_owner + i
        block = ids[k][row * per_owner + i]
        return pltpu.make_async_copy(table.at[block], held.at[n], sems.at[n])

    order = [(k, i) for k in reversed(range(row_count)) for i in range(per_owner)]
    for k, i in order:
        block_of(k, i).start()
    for k, i in order:
        block_of(k, i).wait()
        outs[k][i] = held[k * per_owner + i].astype(jnp.bfloat16)


def pick(row, ids, table, per_owner):
    row_count = len(ids)
    block, rank = table.shape[1:]
    shapes = [VMEM((per_owner, block, rank), jnp.bfloat16)] * row_count
    asked = row_count * per_owner
    return pl.pallas_call(
        functools.partial(pick_kernel, row_count, per_owner),
        out_shape=shapes,
        in_specs=[spec(SMEM)] * (row_count + 1) + [spec(pltpu.HBM)],
        out_specs=[spec(VMEM)] * len(shapes),
        scratch_shapes=[
            VMEM((asked, block, rank), jnp.float32),
            pltpu.SemaphoreType.DMA((asked,)),
        ],
        compiler_params=params(8),
    )(row, *ids, away(table))


def join_kernel(per_owner, first, *refs):
    out = refs[-1]
    out[0:per_owner] = first[...]
    for x in range(1, out.shape[0] // per_owner):
        out[x * per_owner : (x + 1) * per_owner] = refs[x - 1][...]


def join(first, moved, per_owner, marks):
    shape = ((1 + len(moved)) * per_owner,) + first.shape[1:]
    inputs = [first, *moved, *marks]
    return pl.pallas_call(
        functools.partial(join_kernel, per_owner),
        out_shape=VMEM(shape, first.dtype),
        in_specs=[spec(VMEM)] * len(inputs),
        out_specs=spec(VMEM),
        compiler_params=params(1),
    )(*map(near, inputs))


def list_kernel(cfg, row_ref, live_ref, ids_ref, observed, *refs):
    row_count, per_owner, kinds, starts, room = cfg
    pairs_ref, counts_ref, held, mark, sem = refs[-5:]
    mark[...] = jnp.zeros_like(mark)
    copy = pltpu.make_async_copy(observed, held, sem)
    copy.start()
    row = row_ref[0]
    for g in range(len(starts)):
        counts_ref[g] = 0
    for owner in range(row_count):

        @pl.loop(0, live_ref[owner])
        def _(i):
            slot = owner * per_owner + i
            sku_at = (row ^ owner) * per_owner + i
            for n in range(kinds):
                at = ids_ref[slot, n]
                group = jnp.int32(0)
                for start in starts[1:]:
                    group += (at >= start).astype(jnp.int32)
                filled = counts_ref[group]
                pairs_ref[group * room + filled] = at + n * 256 + sku_at * 4096 + slot * 1048576
                counts_ref[group] = filled + 1

    for g, start in enumerate(starts):
        for q in range(batch - 1):
            blank = start + row_count * per_owner * 4096
            pairs_ref[g * room + counts_ref[g] + q] = jnp.int32(blank)
    copy.wait()


def list_pairs(row, live, ids, observed, plan, row_count, per_owner, kinds, marks):
    room = row_count * per_owner * kinds + batch
    groups = len(plan.groups)
    return pl.pallas_call(
        functools.partial(list_kernel, (row_count, per_owner, kinds, plan.starts, room)),
        out_shape=[
            jax.ShapeDtypeStruct((groups * room,), jnp.int32),
            jax.ShapeDtypeStruct((groups,), jnp.int32),
            VMEM(observed.shape, observed.dtype),
            VMEM((8, marks[0].shape[1]), jnp.float32),
        ],
        in_specs=[spec(SMEM)] * 3 + [spec(pltpu.HBM)] + [spec(VMEM)] * len(marks),
        out_specs=[spec(SMEM)] * 2 + [spec(VMEM)] * 2,
        scratch_shapes=[pltpu.SemaphoreType.DMA],
        compiler_params=params(1),
    )(row, live, ids, away(observed), *map(near, marks))


def load_skus(held, refs, starts):
    count = refs[0].shape[0]
    for k, (ref, start) in enumerate(zip(refs, starts)):
        held[pl.ds(k * count, count)] = ref[start : start + count]
    held[len(refs) * count] = jnp.zeros_like(held[0])


def load_table(table, refs):
    at = 0
    for ref in refs:
        table[pl.ds(at, ref.shape[0]), :] = ref[...]
        at += ref.shape[0]


def for_pairs(pairs_ref, counts_ref, room, groups, base, block, body):
    for g in groups:

        @pl.loop(0, pl.cdiv(counts_ref[g], batch))
        def _(b):
            entries = []
            for q in range(batch):
                e = pairs_ref[g * room + b * batch + q]
                at = pl.multiple_of(((e & 255) - base) * block, block)
                entries.append((at, (e >> 8) & 15, (e >> 12) & 255, e >> 20))
            body(entries)


def first_kernel(cfg, pairs_ref, counts_ref, observed, *refs):
    sku_starts, piece_count, out_count, room, groups, base, block = cfg
    sku_count = len(sku_starts)
    skus = refs[:sku_count]
    pieces = refs[sku_count : sku_count + piece_count]
    outs = refs[-3 - out_count : -3]
    held, table, grad = refs[-3:]
    load_skus(held, skus, sku_starts)
    load_table(table, pieces)
    grad[...] = jnp.zeros_like(grad)

    def body(entries):
        terms = []
        for at, n, sku_at, slot in entries:
            sku = held[sku_at]
            predicted = lax.dot_general(
                table[pl.ds(at, block), :], sku, NT, preferred_element_type=jnp.float32
            )
            misfit = predicted - observed[slot, n].T.astype(jnp.float32)
            terms.append(
                jnp.dot(misfit.astype(jnp.bfloat16), sku, preferred_element_type=jnp.float32)
            )
        for (at, _, _, _), term in zip(entries, terms):
            grad[pl.ds(at, block), :] += term

    for_pairs(pairs_ref, counts_ref, room, groups, base, block, body)
    at = 0
    for out in outs:
        out[...] = grad[pl.ds(at, out.shape[0]), :].astype(jnp.bfloat16)
        at += out.shape[0]


def first_pass(pairs, counts, observed, skus, pieces, plan, groups, marks):
    offsets = [d for g in groups for d in plan.groups[g]]
    given = [piece for d in offsets for piece in pieces[d]]
    cuts = [plan.cuts(d) for d in offsets]
    heights = [b - a for spans in cuts for a, b in spans]
    skus, sku_starts = zip(*skus)
    block, rank = plan.block, skus[0].shape[2]
    room = pairs.shape[0] // len(plan.groups)
    slots = len(skus) * skus[0].shape[0]
    cfg = (sku_starts, len(given), len(heights), room, groups, plan.starts[groups[0]], block)
    table = (len(offsets) * plan.rows, rank)
    inputs = [observed, *skus, *given, *marks]
    out = pl.pallas_call(
        functools.partial(first_kernel, cfg),
        out_shape=[VMEM((height, rank), jnp.bfloat16) for height in heights],
        in_specs=[spec(SMEM)] * 2 + [spec(VMEM)] * len(inputs),
        out_specs=[spec(VMEM)] * len(heights),
        scratch_shapes=[
            VMEM((slots + 1, block, rank), jnp.bfloat16),
            VMEM(table, jnp.bfloat16),
            VMEM(table, jnp.float32),
        ],
        compiler_params=params(24),
        cost_estimate=cost(len(offsets) * room // plan.count, block, rank),
    )(pairs, counts, *map(near, inputs))
    out = list(out)
    return {d: [out.pop(0) for _ in spans] for d, spans in zip(offsets, cuts)}


def second_kernel(cfg, pairs_ref, counts_ref, observed, *refs):
    sku_starts, piece_count, room, groups, base, block, begins, ends = cfg
    sku_count = len(sku_starts)
    skus, refs = refs[:sku_count], refs[sku_count:]
    pieces, refs = refs[:piece_count], refs[piece_count:]
    total, mark, *outs = refs[0 if begins else 1 : -2]
    held, table = refs[-2:]
    mark[...] = jnp.zeros_like(mark)
    load_skus(held, skus, sku_starts)
    load_table(table, pieces)
    if begins:
        total[...] = jnp.zeros_like(total)

    def body(entries):
        terms = []
        for at, n, sku_at, slot in entries:
            store = table[pl.ds(at, block), :]
            predicted = lax.dot_general(
                held[sku_at], store, NT, preferred_element_type=jnp.float32
            )
            misfit = predicted - observed[slot, n].astype(jnp.float32)
            terms.append(
                jnp.dot(misfit.astype(jnp.bfloat16), store, preferred_element_type=jnp.float32)
            )
        for (_, _, sku_at, _), term in zip(entries, terms):
            total[sku_at] += term

    for_pairs(pairs_ref, counts_ref, room, groups, base, block, body)
    for k, out in enumerate(outs):
        count = out.shape[0]
        out[...] = total[pl.ds(k * count, count)].astype(jnp.bfloat16)


def second_pass(pairs, counts, observed, skus, pieces, plan, group, total, ends):
    offsets = plan.groups[group]
    given = [piece for d in offsets for piece in pieces[d]]
    skus, sku_starts = zip(*skus)
    block, rank = plan.block, skus[0].shape[2]
    room = pairs.shape[0] // len(plan.groups)
    per_owner = skus[0].shape[0]
    slots = len(skus) * per_owner
    begins = total is None
    cfg = (
        sku_starts, len(given), room, [group], plan.starts[group], block, begins, ends,
    )
    sums = (slots + 1, block, rank)
    out_shape = [VMEM(sums, jnp.float32), VMEM((8, rank), jnp.float32)]
    if ends:
        out_shape += [VMEM((per_owner, block, rank), jnp.bfloat16)] * len(skus)
    inputs = [observed, *skus, *given] + ([] if begins else [total])
    return pl.pallas_call(
        functools.partial(second_kernel, cfg),
        out_shape=out_shape,
        in_specs=[spec(SMEM)] * 2 + [spec(VMEM)] * len(inputs),
        out_specs=[spec(VMEM)] * len(out_shape),
        scratch_shapes=[
            VMEM(sums, jnp.bfloat16),
            VMEM((len(offsets) * plan.rows, rank), jnp.bfloat16),
        ],
        input_output_aliases={} if begins else {1 + len(inputs): 0},
        compiler_params=params(12),
        cost_estimate=cost(len(offsets) * room // plan.count, block, rank),
    )(pairs, counts, *map(near, inputs))


def take_terms(held, ids, terms, row, per_owner):
    blocks = []
    for block_ids, term in zip(ids, terms):
        for i in range(per_owner):
            block = block_ids[row * per_owner + i]
            held[block] -= learn_rate * term[i].astype(jnp.float32)
            blocks.append(block)
    return blocks


def copy_out(held, out, blocks, sems):
    copies = [
        pltpu.make_async_copy(held.at[block], out.at[block], sems.at[n])
        for n, block in enumerate(blocks)
    ]
    for copy in copies:
        copy.start()
    for copy in copies:
        copy.wait()


def base_kernel(count, per_owner, row_ref, *refs):
    ids, sku, terms = refs[:count], refs[count], refs[count + 1 : -3]
    held, out, sems = refs[-3:]
    held[...] = sku[...] * (1.0 - learn_rate * weight_decay)
    take_terms(held, ids, terms, row_ref[0], per_owner)
    copy_out(held, out, range(sku.shape[0]), sems)


def base_step(row, ids, sku, terms, per_owner):
    return pl.pallas_call(
        functools.partial(base_kernel, len(ids), per_owner),
        out_shape=[VMEM(sku.shape, jnp.float32), pltpu.HBM(sku.shape, jnp.float32)],
        in_specs=[spec(SMEM)] * (len(ids) + 1) + [spec(VMEM)] * (1 + len(ids)),
        out_specs=[spec(VMEM), spec(pltpu.HBM)],
        scratch_shapes=[pltpu.SemaphoreType.DMA((sku.shape[0],))],
        compiler_params=params(8),
    )(row, *ids, sku, *map(near, terms))


def finish_kernel(count, per_owner, row_ref, *refs):
    ids, sku, terms = refs[:count], refs[count], refs[count + 1 : 2 * count + 1]
    out, held, sems = refs[-3:]
    for block_ids in ids:
        for i in range(per_owner):
            block = block_ids[row_ref[0] * per_owner + i]
            held[block] = sku[block]
    blocks = take_terms(held, ids, terms, row_ref[0], per_owner)
    copy_out(held, out, blocks, sems)


def finish_step(row, ids, held, out, terms, per_owner):
    return pl.pallas_call(
        functools.partial(finish_kernel, len(ids), per_owner),
        out_shape=pltpu.HBM(out.shape, jnp.float32),
        in_specs=[spec(SMEM)] * (len(ids) + 1)
        + [spec(VMEM)] * (1 + len(ids))
        + [spec(pltpu.HBM)],
        out_specs=spec(pltpu.HBM),
        scratch_shapes=[
            VMEM(out.shape, jnp.float32),
            pltpu.SemaphoreType.DMA((len(ids) * per_owner,)),
        ],
        input_output_aliases={2 + 2 * len(ids): 0},
        compiler_params=params(4),
    )(row, *ids, near(held), *map(near, terms), away(out))


def local(observed, sku_ids, store_ids, live_slot_counts, sku_factors, store_factors):
    row_count = lax.axis_size("row")
    per_owner = observed.shape[0] // row_count
    kinds, block = observed.shape[1:3]
    rank = sku_factors.shape[1]
    plan = Plan(lax.axis_size("col"), store_factors.shape[0], block)
    row_vec = lax.axis_index("row").reshape(1).astype(jnp.int32)
    live = live_slot_counts.reshape(row_count)
    sku = sku_factors.reshape(-1, block, rank)

    swaps = [[(r, r ^ k) for r in range(row_count)] for k in range(row_count)]
    asked = [sku_ids] + [lax.ppermute(sku_ids, "row", swaps[k]) for k in range(1, row_count)]
    picked = pick(row_vec, asked, sku, per_owner)
    place = ring_place(lax.axis_index("col"), plan.count)
    owner_place = ring_place(store_ids // plan.blocks, plan.count)
    arrival = plan.arrival((owner_place - place) % plan.count)
    ids = arrival * plan.blocks + store_ids % plan.blocks
    pieces = gather_ring(store_factors.astype(jnp.bfloat16), plan)
    early = pieces[1] + pieces[plan.count - 1]
    pairs, counts, observed, listed = list_pairs(
        row_vec, live, ids, observed, plan, row_count, per_owner, kinds, early
    )

    direct, through = [], []
    for x in range(1, row_count // 2):
        direct.append(lax.ppermute(picked[2 * x], "row", swaps[2 * x]))
        onward = after(after(picked[2 * x + 1], direct[-1][0]), listed)
        through.append(lax.ppermute(onward, "row", swaps[2 * x]))
    late = pieces[plan.far - 1] + pieces[plan.far + 1]
    passed = lax.ppermute(join(picked[1], through, per_owner, late), "row", swaps[1])
    skus = [(picked[0], 0), (passed, 0)]
    for x, blocks in enumerate(direct, 1):
        skus += [(blocks, 0), (passed, x * per_owner)]

    grads, marks = {}, []
    for group in (2, 3, 1, 0):
        if plan.groups[group]:
            some = first_pass(pairs, counts, observed, skus, pieces, plan, [group], marks)
            grads.update(some)
            marks = some[plan.groups[group][0]][:1]
    own_grad = scatter_ring(grads, plan)
    new_store = store_factors - learn_rate * (own_grad + weight_decay * store_factors)
    made, ties = [], {}

    def add_group(step, pieces):
        due = {1: 0, plan.far - 2: 1, plan.far - 1: 2, plan.far: 3}
        if step in due:
            group = due[step]
            total = made[-1][0] if made else None
            made.append(
                second_pass(
                    pairs, counts, observed, skus, pieces, plan, group, total, group == 3
                )
            )
            if group < 2:
                ties[step + 2] = made[-1][1]

    gather_ring(new_store.astype(jnp.bfloat16), plan, ties, add_group)
    out = made[-1][2:]
    terms = [out[0]] + [lax.ppermute(out[k], "row", swaps[k]) for k in range(1, row_count)]
    held, new_sku = base_step(row_vec, asked[:2], sku, terms[:2], per_owner)
    new_sku = finish_step(row_vec, asked[2:], held, new_sku, terms[2:], per_owner)
    return new_sku.reshape(sku_factors.shape), new_store


def solution(mesh):
    placed = (
        P(("row", "col"), None, None, None),
        P(("row", "col")),
        P(("row", "col"), None),
        P("row", "col", None),
        P(("row", "col"), None),
        P(("row", "col"), None),
    )
    return jax.shard_map(
        local,
        mesh=mesh,
        in_specs=placed,
        out_specs=(P(("row", "col"), None), P(("row", "col"), None)),
        check_vma=False,
    )
```

```python
import functools

import jax
import jax.numpy as jnp
from jax import lax
from jax.experimental import pallas as pl
from jax.experimental.pallas import tpu as pltpu
from jax.sharding import PartitionSpec as P

learn_rate = 0.01
weight_decay = 0.05
line_len = 4
batch = 8
split_sum = False
split_gather = True

VMEM = pltpu.VMEM
SMEM = pltpu.SMEM
NT = (((1,), (1,)), ((), ()))


def spec(space):
    return pl.BlockSpec(memory_space=space)


def near(array):
    return pltpu.with_memory_space_constraint(array, VMEM)


def away(array):
    return pltpu.with_memory_space_constraint(array, pltpu.HBM)


def params(mib):
    return pltpu.CompilerParams(vmem_limit_bytes=mib * 1024 * 1024)


def cost(pairs, block, rank):
    return pl.CostEstimate(
        flops=pairs * 4 * block * block * rank,
        bytes_accessed=pairs * 256 * 1024,
        transcendentals=0,
    )


def ring_place(col, col_count):
    width = max(col_count // line_len, 1)
    depth = col_count // width
    across, along = col % width, col // width
    return across * depth + jnp.where(across % 2 == 0, along, depth - 1 - along)


def ring_steps(col_count):
    width = max(col_count // line_len, 1)
    depth = col_count // width
    order = []
    for place in range(col_count):
        across, along = divmod(place, depth)
        along = along if across % 2 == 0 else depth - 1 - along
        order.append(along * width + across)
    ahead = [(order[p], order[(p + 1) % col_count]) for p in range(col_count)]
    back = [(b, a) for a, b in ahead]
    return ahead, back


class Plan:
    def __init__(self, col_count, rows, block):
        self.count = col_count
        self.far = col_count // 2
        self.rows, self.block = rows, block
        self.blocks = rows // block
        first = (self.blocks + 1) // 2 * block
        self.halves = [(0, first), (first, rows)]
        self.order = [0]
        for m in range(1, self.far):
            self.order += [m, col_count - m]
        self.order.append(self.far)
        self.groups = [self.order[:3], self.order[3:-3], self.order[-3:-1], self.order[-1:]]
        self.starts = [self.order.index(g[0]) * self.blocks for g in self.groups]

    def arrival(self, offset):
        back = self.count - offset
        return jnp.where(
            offset == 0,
            0,
            jnp.where(
                offset == self.far,
                self.count - 1,
                jnp.where(offset < self.far, 2 * offset - 1, 2 * back),
            ),
        )

    def cuts(self, offset):
        return self.halves if split_sum or offset == self.far else [(0, self.rows)]


def after(value, mark):
    return jnp.where(mark[:1] < jnp.inf, value, jnp.zeros_like(value))


def gather_ring(low, plan, marks=None, arrived=None):
    steps = ring_steps(plan.count)
    moved = [low, low]
    pieces = {0: [low]}
    for step in range(1, plan.far + 1):
        if step == plan.far:
            moved = [moved[way][a:b] for way, (a, b) in enumerate(plan.halves)]
        if marks is not None and step in marks:
            moved = [after(value, marks[step]) for value in moved]
        moved = [lax.ppermute(moved[way], "col", steps[way]) for way in (0, 1)]
        if step == plan.far:
            pieces[step] = moved
        else:
            pieces[plan.count - step] = moved[:1]
            pieces[step] = moved[1:]
        if arrived:
            arrived(step, pieces)
    return pieces


def gather_split(low, plan):
    steps = ring_steps(plan.count)
    parts = [low[a:b] for a, b in plan.halves]
    moved = {(way, h): parts[h] for way in (0, 1) for h in (0, 1)}
    pieces = {offset: [None, None] for offset in plan.order}
    pieces[0] = parts
    for step in range(1, plan.far + 1):
        for h in (0, 1):
            for way in (0, 1):
                if step < plan.far or way == h:
                    moved[way, h] = lax.ppermute(moved[way, h], "col", steps[way])
                    pieces[step if way else plan.count - step][h] = moved[way, h]
    return pieces


def add_up(moved, piece):
    return (moved.astype(jnp.float32) + piece.astype(jnp.float32)).astype(jnp.bfloat16)


def scatter_ring(pieces, plan):
    steps = ring_steps(plan.count)
    first = plan.halves[0][1]
    moved = [lax.ppermute(pieces[plan.far][way], "col", steps[way]) for way in (0, 1)]
    for step in range(plan.far - 1, 0, -1):
        for way in (0, 1):
            (value,) = pieces[plan.count - step if way else step]
            if step == plan.far - 1:
                parts = [value[:first], value[first:]]
                parts[way] = add_up(moved[way], parts[way])
                value = jnp.concatenate(parts, axis=0)
            else:
                value = add_up(moved[way], value)
            moved[way] = lax.ppermute(value, "col", steps[way])
    return (
        pieces[0][0].astype(jnp.float32)
        + moved[0].astype(jnp.float32)
        + moved[1].astype(jnp.float32)
    )


def scatter_split(pieces, plan):
    steps = ring_steps(plan.count)
    moved = {}
    for step in range(plan.far, 0, -1):
        for h in (0, 1):
            for way in (0, 1):
                if step < plan.far or way == h:
                    value = pieces[plan.count - step if way else step][h]
                    if (way, h) in moved:
                        value = add_up(moved[way, h], value)
                    moved[way, h] = lax.ppermute(value, "col", steps[way])
    return jnp.concatenate(
        [
            pieces[0][h].astype(jnp.float32)
            + moved[0, h].astype(jnp.float32)
            + moved[1, h].astype(jnp.float32)
            for h in (0, 1)
        ],
        axis=0,
    )


def pick_kernel(row_count, per_owner, row_ref, *refs):
    ids = refs[:row_count]
    table, _, *outs = refs[row_count:-2]
    held, sems = refs[-2:]
    row = row_ref[0]

    def block_of(k, i):
        n = k * per_owner + i
        block = ids[k][row * per_owner + i]
        return pltpu.make_async_copy(table.at[block], held.at[n], sems.at[n])

    order = [(k, i) for k in reversed(range(row_count)) for i in range(per_owner)]
    for k, i in order:
        block_of(k, i).start()
    for k, i in order:
        block_of(k, i).wait()
        outs[k][i] = held[k * per_owner + i].astype(jnp.bfloat16)


def pick(row, ids, table, per_owner, mark):
    row_count = len(ids)
    block, rank = table.shape[1:]
    shapes = [VMEM((per_owner, block, rank), jnp.bfloat16)] * row_count
    asked = row_count * per_owner
    return pl.pallas_call(
        functools.partial(pick_kernel, row_count, per_owner),
        out_shape=shapes,
        in_specs=[spec(SMEM)] * (row_count + 1) + [spec(pltpu.HBM), spec(VMEM)],
        out_specs=[spec(VMEM)] * len(shapes),
        scratch_shapes=[
            VMEM((asked, block, rank), jnp.float32),
            pltpu.SemaphoreType.DMA((asked,)),
        ],
        compiler_params=params(8),
    )(row, *ids, away(table), near(mark))


def join_kernel(per_owner, first, *refs):
    out = refs[-1]
    out[0:per_owner] = first[...]
    for x in range(1, out.shape[0] // per_owner):
        out[x * per_owner : (x + 1) * per_owner] = refs[x - 1][...]


def join(first, moved, per_owner, marks):
    shape = ((1 + len(moved)) * per_owner,) + first.shape[1:]
    inputs = [first, *moved, *marks]
    return pl.pallas_call(
        functools.partial(join_kernel, per_owner),
        out_shape=VMEM(shape, first.dtype),
        in_specs=[spec(VMEM)] * len(inputs),
        out_specs=spec(VMEM),
        compiler_params=params(1),
    )(*map(near, inputs))


def list_kernel(cfg, row_ref, live_ref, ids_ref, observed, *refs):
    row_count, per_owner, kinds, starts, room = cfg
    pairs_ref, counts_ref, held, mark, sem = refs[-5:]
    mark[...] = jnp.zeros_like(mark)
    copy = pltpu.make_async_copy(observed, held, sem)
    copy.start()
    row = row_ref[0]
    counts = (jnp.int32(0),) * len(starts)
    for owner in range(row_count):

        def add_slot(i, counts):
            slot = owner * per_owner + i
            sku_at = (row ^ owner) * per_owner + i
            tag = sku_at * 4096 + slot * 1048576
            for n in range(kinds):
                at = ids_ref[n, slot]
                group, filled = jnp.int32(0), counts[0]
                for g, start in enumerate(starts[1:], 1):
                    group = jnp.where(at >= start, g, group)
                    filled = jnp.where(at >= start, counts[g], filled)
                pairs_ref[group * room + filled] = at + n * 256 + tag
                counts = tuple(
                    count + (group == g).astype(jnp.int32) for g, count in enumerate(counts)
                )
            return counts

        counts = lax.fori_loop(0, live_ref[owner], add_slot, counts)

    for g, count in enumerate(counts):
        counts_ref[g] = count
    for g, start in enumerate(starts):
        for q in range(batch - 1):
            blank = start + row_count * per_owner * 4096
            pairs_ref[g * room + counts[g] + q] = jnp.int32(blank)
    copy.wait()


def list_pairs(row, live, ids, observed, plan, row_count, per_owner, kinds, rank):
    room = row_count * per_owner * kinds + batch
    groups = len(plan.groups)
    return pl.pallas_call(
        functools.partial(list_kernel, (row_count, per_owner, kinds, plan.starts, room)),
        out_shape=[
            jax.ShapeDtypeStruct((groups * room,), jnp.int32),
            jax.ShapeDtypeStruct((groups,), jnp.int32),
            VMEM(observed.shape, observed.dtype),
            VMEM((8, rank), jnp.float32),
        ],
        in_specs=[spec(SMEM)] * 3 + [spec(pltpu.HBM)],
        out_specs=[spec(SMEM)] * 2 + [spec(VMEM)] * 2,
        scratch_shapes=[pltpu.SemaphoreType.DMA],
        compiler_params=params(1),
    )(row, live, ids, away(observed))


def load_skus(held, refs, starts):
    count = refs[0].shape[0]
    for k, (ref, start) in enumerate(zip(refs, starts)):
        held[pl.ds(k * count, count)] = ref[start : start + count]
    held[len(refs) * count] = jnp.zeros_like(held[0])


def load_table(table, refs):
    at = 0
    for ref in refs:
        table[pl.ds(at, ref.shape[0]), :] = ref[...]
        at += ref.shape[0]


def for_pairs(pairs_ref, counts_ref, room, groups, base, block, body):
    for g in groups:

        @pl.loop(0, pl.cdiv(counts_ref[g], batch))
        def _(b):
            entries = []
            for q in range(batch):
                e = pairs_ref[g * room + b * batch + q]
                at = pl.multiple_of(((e & 255) - base) * block, block)
                entries.append((at, (e >> 8) & 15, (e >> 12) & 255, e >> 20))
            body(entries)


def first_kernel(cfg, pairs_ref, counts_ref, observed, *refs):
    sku_starts, piece_count, out_count, room, groups, base, block = cfg
    sku_count = len(sku_starts)
    skus = refs[:sku_count]
    pieces = refs[sku_count : sku_count + piece_count]
    outs = refs[-3 - out_count : -3]
    held, table, grad = refs[-3:]
    load_skus(held, skus, sku_starts)
    load_table(table, pieces)
    grad[...] = jnp.zeros_like(grad)

    def body(entries):
        terms = []
        for at, n, sku_at, slot in entries:
            sku = held[sku_at]
            predicted = lax.dot_general(
                table[pl.ds(at, block), :], sku, NT, preferred_element_type=jnp.float32
            )
            misfit = predicted - observed[slot, n].T.astype(jnp.float32)
            terms.append(
                jnp.dot(misfit.astype(jnp.bfloat16), sku, preferred_element_type=jnp.float32)
            )
        for (at, _, _, _), term in zip(entries, terms):
            grad[pl.ds(at, block), :] += term

    for_pairs(pairs_ref, counts_ref, room, groups, base, block, body)
    at = 0
    for out in outs:
        out[...] = grad[pl.ds(at, out.shape[0]), :].astype(jnp.bfloat16)
        at += out.shape[0]


def first_pass(pairs, counts, observed, skus, pieces, plan, groups, marks):
    offsets = [d for g in groups for d in plan.groups[g]]
    given = [piece for d in offsets for piece in pieces[d]]
    cuts = [plan.cuts(d) for d in offsets]
    heights = [b - a for spans in cuts for a, b in spans]
    skus, sku_starts = zip(*skus)
    block, rank = plan.block, skus[0].shape[2]
    room = pairs.shape[0] // len(plan.groups)
    slots = len(skus) * skus[0].shape[0]
    cfg = (sku_starts, len(given), len(heights), room, groups, plan.starts[groups[0]], block)
    table = (len(offsets) * plan.rows, rank)
    inputs = [observed, *skus, *given, *marks]
    out = pl.pallas_call(
        functools.partial(first_kernel, cfg),
        out_shape=[VMEM((height, rank), jnp.bfloat16) for height in heights],
        in_specs=[spec(SMEM)] * 2 + [spec(VMEM)] * len(inputs),
        out_specs=[spec(VMEM)] * len(heights),
        scratch_shapes=[
            VMEM((slots + 1, block, rank), jnp.bfloat16),
            VMEM(table, jnp.bfloat16),
            VMEM(table, jnp.float32),
        ],
        compiler_params=params(24),
        cost_estimate=cost(len(offsets) * room // plan.count, block, rank),
    )(pairs, counts, *map(near, inputs))
    out = list(out)
    return {d: [out.pop(0) for _ in spans] for d, spans in zip(offsets, cuts)}


def second_kernel(cfg, row_ref, live_ref, ids_ref, observed, *refs):
    ks, sku_starts, per_owner, kinds, block = cfg
    skus, pieces = refs[: len(ks)], refs[len(ks) : -1 - len(ks)]
    outs, table = refs[-1 - len(ks) : -1], refs[-1]
    load_table(table, pieces)
    row = row_ref[0]
    for k, sku_ref, start, out in zip(ks, skus, sku_starts, outs):
        out[...] = jnp.zeros_like(out)
        owner = row ^ k

        @pl.loop(0, live_ref[owner])
        def _(i):
            slot = owner * per_owner + i
            stores, measured = [], []
            for n in range(kinds):
                at = pl.multiple_of(ids_ref[n, slot] * block, block)
                stores.append(table[pl.ds(at, block), :])
                measured.append(observed[slot, n])
            store = jnp.concatenate(stores, axis=0)
            predicted = lax.dot_general(
                sku_ref[start + i], store, NT, preferred_element_type=jnp.float32
            )
            misfit = predicted - jnp.concatenate(measured, axis=1).astype(jnp.float32)
            out[i] = jnp.dot(
                misfit.astype(jnp.bfloat16), store, preferred_element_type=jnp.float32
            ).astype(jnp.bfloat16)


def second_pass(ks, row, live, ids, observed, skus, pieces, plan, per_owner):
    kept, sku_starts = zip(*[skus[k] for k in ks])
    kinds, block, rank = observed.shape[1], plan.block, kept[0].shape[2]
    shape = (per_owner, block, rank)
    inputs = [observed, *kept, *[piece for d in plan.order for piece in pieces[d]]]
    return pl.pallas_call(
        functools.partial(second_kernel, (ks, sku_starts, per_owner, kinds, block)),
        out_shape=[VMEM(shape, jnp.bfloat16)] * len(ks),
        in_specs=[spec(SMEM)] * 3 + [spec(VMEM)] * len(inputs),
        out_specs=[spec(VMEM)] * len(ks),
        scratch_shapes=[VMEM((plan.count * plan.rows, rank), jnp.bfloat16)],
        compiler_params=params(16),
        cost_estimate=cost(len(ks) * per_owner * kinds, block, rank),
    )(row, live, ids, *map(near, inputs))


def take_terms(held, ids, terms, row, per_owner):
    blocks = []
    for block_ids, term in zip(ids, terms):
        for i in range(per_owner):
            block = block_ids[row * per_owner + i]
            held[block] -= learn_rate * term[i].astype(jnp.float32)
            blocks.append(block)
    return blocks


def copy_out(held, out, blocks, sems):
    copies = [
        pltpu.make_async_copy(held.at[block], out.at[block], sems.at[n])
        for n, block in enumerate(blocks)
    ]
    for copy in copies:
        copy.start()
    for copy in copies:
        copy.wait()


def base_kernel(count, per_owner, row_ref, *refs):
    ids, sku, terms = refs[:count], refs[count], refs[count + 1 : -3]
    held, out, sems = refs[-3:]
    held[...] = sku[...] * (1.0 - learn_rate * weight_decay)
    take_terms(held, ids, terms, row_ref[0], per_owner)
    copy_out(held, out, range(sku.shape[0]), sems)


def base_step(row, ids, sku, terms, per_owner):
    return pl.pallas_call(
        functools.partial(base_kernel, len(ids), per_owner),
        out_shape=[VMEM(sku.shape, jnp.float32), pltpu.HBM(sku.shape, jnp.float32)],
        in_specs=[spec(SMEM)] * (len(ids) + 1) + [spec(VMEM)] * (1 + len(ids)),
        out_specs=[spec(VMEM), spec(pltpu.HBM)],
        scratch_shapes=[pltpu.SemaphoreType.DMA((sku.shape[0],))],
        compiler_params=params(8),
    )(row, *ids, sku, *map(near, terms))


def finish_kernel(count, per_owner, row_ref, *refs):
    ids, sku, terms = refs[:count], refs[count], refs[count + 1 : 2 * count + 1]
    out, held, sems = refs[-3:]
    for block_ids in ids:
        for i in range(per_owner):
            block = block_ids[row_ref[0] * per_owner + i]
            held[block] = sku[block]
    blocks = take_terms(held, ids, terms, row_ref[0], per_owner)
    copy_out(held, out, blocks, sems)


def finish_step(row, ids, held, out, terms, per_owner):
    return pl.pallas_call(
        functools.partial(finish_kernel, len(ids), per_owner),
        out_shape=pltpu.HBM(out.shape, jnp.float32),
        in_specs=[spec(SMEM)] * (len(ids) + 1)
        + [spec(VMEM)] * (1 + len(ids))
        + [spec(pltpu.HBM)],
        out_specs=spec(pltpu.HBM),
        scratch_shapes=[
            VMEM(out.shape, jnp.float32),
            pltpu.SemaphoreType.DMA((len(ids) * per_owner,)),
        ],
        input_output_aliases={2 + 2 * len(ids): 0},
        compiler_params=params(4),
    )(row, *ids, near(held), *map(near, terms), away(out))


def local(observed, sku_ids, store_ids, live_slot_counts, sku_factors, store_factors):
    row_count = lax.axis_size("row")
    per_owner = observed.shape[0] // row_count
    kinds, block = observed.shape[1:3]
    rank = sku_factors.shape[1]
    plan = Plan(lax.axis_size("col"), store_factors.shape[0], block)
    row_vec = lax.axis_index("row").reshape(1).astype(jnp.int32)
    live = live_slot_counts.reshape(row_count)
    sku = sku_factors.reshape(-1, block, rank)

    swaps = [[(r, r ^ k) for r in range(row_count)] for k in range(row_count)]
    asked = [sku_ids] + [lax.ppermute(sku_ids, "row", swaps[k]) for k in range(1, row_count)]
    place = ring_place(lax.axis_index("col"), plan.count)
    store_ids = store_ids.T
    owner_place = ring_place(store_ids // plan.blocks, plan.count)
    arrival = plan.arrival((owner_place - place) % plan.count)
    ids = arrival * plan.blocks + store_ids % plan.blocks
    pairs, counts, observed, listed = list_pairs(
        row_vec, live, ids, observed, plan, row_count, per_owner, kinds, rank
    )
    picked = pick(row_vec, asked, sku, per_owner, listed)
    pieces = gather_ring(store_factors.astype(jnp.bfloat16), plan)

    direct, through = [], []
    for x in range(1, row_count // 2):
        direct.append(lax.ppermute(picked[2 * x], "row", swaps[2 * x]))
        onward = after(picked[2 * x + 1], direct[-1][0])
        through.append(lax.ppermute(onward, "row", swaps[2 * x]))
    late = pieces[plan.far - 1] + pieces[plan.far + 1]
    passed = lax.ppermute(join(picked[1], through, per_owner, late), "row", swaps[1])
    skus = [(picked[0], 0), (passed, 0)]
    for x, blocks in enumerate(direct, 1):
        skus += [(blocks, 0), (passed, x * per_owner)]

    grads, marks = {}, []
    for group in (2, 3, 1, 0):
        if plan.groups[group]:
            some = first_pass(pairs, counts, observed, skus, pieces, plan, [group], marks)
            grads.update(some)
            marks = some[plan.groups[group][0]][:1]
    own_grad = (scatter_split if split_sum else scatter_ring)(grads, plan)

    def step_of(grad):
        return store_factors - learn_rate * (grad + weight_decay * store_factors)

    new_low = step_of(own_grad).astype(jnp.bfloat16)
    new_pieces = (gather_split if split_gather else gather_ring)(new_low, plan)

    terms = [None] * row_count
    for ks in (list(range(2, row_count)), [1, 0]):
        out = second_pass(ks, row_vec, live, ids, observed, skus, new_pieces, plan, per_owner)
        for k, term in zip(ks, out):
            terms[k] = lax.ppermute(term, "row", swaps[k]) if k else term
    held, new_sku = base_step(row_vec, asked[:2], sku, terms[:2], per_owner)
    new_sku = finish_step(row_vec, asked[2:], held, new_sku, terms[2:], per_owner)
    new_store = step_of(after(own_grad, new_pieces[plan.far][1]))
    return new_sku.reshape(sku_factors.shape), new_store


def solution(mesh):
    placed = (
        P(("row", "col"), None, None, None),
        P(("row", "col")),
        P(("row", "col"), None),
        P("row", "col", None),
        P(("row", "col"), None),
        P(("row", "col"), None),
    )
    return jax.shard_map(
        local,
        mesh=mesh,
        in_specs=placed,
        out_specs=(P(("row", "col"), None), P(("row", "col"), None)),
        check_vma=False,
    )
```

```python
import functools

import jax
import jax.numpy as jnp
from jax import lax
from jax.experimental import pallas as pl
from jax.experimental.pallas import tpu as pltpu
from jax.sharding import PartitionSpec as P

learn_rate = 0.01
weight_decay = 0.05
line_len = 4
batch = 8
split_sum = False
split_gather = True

VMEM = pltpu.VMEM
SMEM = pltpu.SMEM
NT = (((1,), (1,)), ((), ()))


def spec(space):
    return pl.BlockSpec(memory_space=space)


def near(array):
    return pltpu.with_memory_space_constraint(array, VMEM)


def away(array):
    return pltpu.with_memory_space_constraint(array, pltpu.HBM)


def params(mib):
    return pltpu.CompilerParams(vmem_limit_bytes=mib * 1024 * 1024)


def cost(pairs, block, rank):
    return pl.CostEstimate(
        flops=pairs * 4 * block * block * rank,
        bytes_accessed=pairs * 256 * 1024,
        transcendentals=0,
    )


def ring_place(col, col_count):
    width = max(col_count // line_len, 1)
    depth = col_count // width
    across, along = col % width, col // width
    return across * depth + jnp.where(across % 2 == 0, along, depth - 1 - along)


def ring_steps(col_count):
    width = max(col_count // line_len, 1)
    depth = col_count // width
    order = []
    for place in range(col_count):
        across, along = divmod(place, depth)
        along = along if across % 2 == 0 else depth - 1 - along
        order.append(along * width + across)
    ahead = [(order[p], order[(p + 1) % col_count]) for p in range(col_count)]
    back = [(b, a) for a, b in ahead]
    return ahead, back


class Plan:
    def __init__(self, col_count, rows, block):
        self.count = col_count
        self.far = col_count // 2
        self.rows, self.block = rows, block
        self.blocks = rows // block
        first = (self.blocks + 1) // 2 * block
        self.halves = [(0, first), (first, rows)]
        self.order = [0]
        for m in range(1, self.far):
            self.order += [m, col_count - m]
        self.order.append(self.far)
        self.groups = [self.order[:3], self.order[3:-3], self.order[-3:-1], self.order[-1:]]
        self.starts = [self.order.index(g[0]) * self.blocks for g in self.groups]

    def arrival(self, offset):
        back = self.count - offset
        return jnp.where(
            offset == 0,
            0,
            jnp.where(
                offset == self.far,
                self.count - 1,
                jnp.where(offset < self.far, 2 * offset - 1, 2 * back),
            ),
        )

    def cuts(self, offset):
        return self.halves if split_sum or offset == self.far else [(0, self.rows)]


def after(value, mark):
    return jnp.where(mark[:1] < jnp.inf, value, jnp.zeros_like(value))


def gather_ring(low, plan, marks=None, arrived=None):
    steps = ring_steps(plan.count)
    moved = [low, low]
    pieces = {0: [low]}
    for step in range(1, plan.far + 1):
        if step == plan.far:
            moved = [moved[way][a:b] for way, (a, b) in enumerate(plan.halves)]
        if marks is not None and step in marks:
            moved = [after(value, marks[step]) for value in moved]
        moved = [lax.ppermute(moved[way], "col", steps[way]) for way in (0, 1)]
        if step == plan.far:
            pieces[step] = moved
        else:
            pieces[plan.count - step] = moved[:1]
            pieces[step] = moved[1:]
        if arrived:
            arrived(step, pieces)
    return pieces


def gather_split(low, plan):
    steps = ring_steps(plan.count)
    parts = [low[a:b] for a, b in plan.halves]
    moved = {(way, h): parts[h] for way in (0, 1) for h in (0, 1)}
    pieces = {offset: [None, None] for offset in plan.order}
    pieces[0] = parts
    for step in range(1, plan.far + 1):
        for h in (0, 1):
            for way in (0, 1):
                if step < plan.far or way == h:
                    moved[way, h] = lax.ppermute(moved[way, h], "col", steps[way])
                    pieces[step if way else plan.count - step][h] = moved[way, h]
    return pieces


def add_up(moved, piece):
    return (moved.astype(jnp.float32) + piece.astype(jnp.float32)).astype(jnp.bfloat16)


def scatter_ring(pieces, plan):
    steps = ring_steps(plan.count)
    first = plan.halves[0][1]
    moved = [lax.ppermute(pieces[plan.far][way], "col", steps[way]) for way in (0, 1)]
    for step in range(plan.far - 1, 0, -1):
        for way in (0, 1):
            (value,) = pieces[plan.count - step if way else step]
            if step == plan.far - 1:
                parts = [value[:first], value[first:]]
                parts[way] = add_up(moved[way], parts[way])
                value = jnp.concatenate(parts, axis=0)
            else:
                value = add_up(moved[way], value)
            moved[way] = lax.ppermute(value, "col", steps[way])
    return (
        pieces[0][0].astype(jnp.float32)
        + moved[0].astype(jnp.float32)
        + moved[1].astype(jnp.float32)
    )


def scatter_split(pieces, plan):
    steps = ring_steps(plan.count)
    moved = {}
    for step in range(plan.far, 0, -1):
        for h in (0, 1):
            for way in (0, 1):
                if step < plan.far or way == h:
                    value = pieces[plan.count - step if way else step][h]
                    if (way, h) in moved:
                        value = add_up(moved[way, h], value)
                    moved[way, h] = lax.ppermute(value, "col", steps[way])
    return jnp.concatenate(
        [
            pieces[0][h].astype(jnp.float32)
            + moved[0, h].astype(jnp.float32)
            + moved[1, h].astype(jnp.float32)
            for h in (0, 1)
        ],
        axis=0,
    )


def pick_kernel(row_count, per_owner, row_ref, *refs):
    ids = refs[:row_count]
    table, _, *outs = refs[row_count:-2]
    held, sems = refs[-2:]
    row = row_ref[0]

    def block_of(k, i):
        n = k * per_owner + i
        block = ids[k][row * per_owner + i]
        return pltpu.make_async_copy(table.at[block], held.at[n], sems.at[n])

    order = [(k, i) for k in reversed(range(row_count)) for i in range(per_owner)]
    for k, i in order:
        block_of(k, i).start()
    for k, i in order:
        block_of(k, i).wait()
        outs[k][i] = held[k * per_owner + i].astype(jnp.bfloat16)


def pick(row, ids, table, per_owner, mark):
    row_count = len(ids)
    block, rank = table.shape[1:]
    shapes = [VMEM((per_owner, block, rank), jnp.bfloat16)] * row_count
    asked = row_count * per_owner
    return pl.pallas_call(
        functools.partial(pick_kernel, row_count, per_owner),
        out_shape=shapes,
        in_specs=[spec(SMEM)] * (row_count + 1) + [spec(pltpu.HBM), spec(VMEM)],
        out_specs=[spec(VMEM)] * len(shapes),
        scratch_shapes=[
            VMEM((asked, block, rank), jnp.float32),
            pltpu.SemaphoreType.DMA((asked,)),
        ],
        compiler_params=params(8),
    )(row, *ids, away(table), near(mark))


def join_kernel(per_owner, first, *refs):
    out = refs[-1]
    out[0:per_owner] = first[...]
    for x in range(1, out.shape[0] // per_owner):
        out[x * per_owner : (x + 1) * per_owner] = refs[x - 1][...]


def join(first, moved, per_owner, marks):
    shape = ((1 + len(moved)) * per_owner,) + first.shape[1:]
    inputs = [first, *moved, *marks]
    return pl.pallas_call(
        functools.partial(join_kernel, per_owner),
        out_shape=VMEM(shape, first.dtype),
        in_specs=[spec(VMEM)] * len(inputs),
        out_specs=spec(VMEM),
        compiler_params=params(1),
    )(*map(near, inputs))


def list_kernel(cfg, row_ref, live_ref, ids_ref, pairs_ref, counts_ref, mark):
    row_count, per_owner, kinds, starts, room = cfg
    mark[...] = jnp.zeros_like(mark)
    row = row_ref[0]
    counts = (jnp.int32(0),) * len(starts)
    for owner in range(row_count):

        def add_slot(i, counts):
            slot = owner * per_owner + i
            sku_at = (row ^ owner) * per_owner + i
            tag = sku_at * 4096 + slot * 1048576
            for n in range(kinds):
                at = ids_ref[n, slot]
                group, filled = jnp.int32(0), counts[0]
                for g, start in enumerate(starts[1:], 1):
                    group = jnp.where(at >= start, g, group)
                    filled = jnp.where(at >= start, counts[g], filled)
                pairs_ref[group * room + filled] = at + n * 256 + tag
                counts = tuple(
                    count + (group == g).astype(jnp.int32) for g, count in enumerate(counts)
                )
            return counts

        counts = lax.fori_loop(0, live_ref[owner], add_slot, counts)

    for g, count in enumerate(counts):
        counts_ref[g] = count
    for g, start in enumerate(starts):
        for q in range(batch - 1):
            blank = start + row_count * per_owner * 4096
            pairs_ref[g * room + counts[g] + q] = jnp.int32(blank)


def list_pairs(row, live, ids, plan, row_count, per_owner, kinds, rank):
    room = row_count * per_owner * kinds + batch
    groups = len(plan.groups)
    return pl.pallas_call(
        functools.partial(list_kernel, (row_count, per_owner, kinds, plan.starts, room)),
        out_shape=[
            jax.ShapeDtypeStruct((groups * room,), jnp.int32),
            jax.ShapeDtypeStruct((groups,), jnp.int32),
            VMEM((8, rank), jnp.float32),
        ],
        in_specs=[spec(SMEM)] * 3,
        out_specs=[spec(SMEM)] * 2 + [spec(VMEM)],
        compiler_params=params(1),
    )(row, live, ids)


def hold_kernel(observed, *refs):
    held, mark, sems = refs[-3:]
    copies = [
        pltpu.make_async_copy(observed.at[slot], held.at[slot], sems.at[slot])
        for slot in range(observed.shape[0])
    ]
    for copy in copies:
        copy.start()
    mark[...] = jnp.zeros_like(mark)
    for copy in copies:
        copy.wait()


def hold(observed, marks):
    return pl.pallas_call(
        hold_kernel,
        out_shape=[
            VMEM(observed.shape, observed.dtype),
            VMEM((8, marks[0].shape[1]), jnp.float32),
        ],
        in_specs=[spec(pltpu.HBM)] + [spec(VMEM)] * len(marks),
        out_specs=[spec(VMEM)] * 2,
        scratch_shapes=[pltpu.SemaphoreType.DMA((observed.shape[0],))],
        compiler_params=params(1),
    )(away(observed), *map(near, marks))


def load_skus(held, refs, starts):
    count = refs[0].shape[0]
    for k, (ref, start) in enumerate(zip(refs, starts)):
        held[pl.ds(k * count, count)] = ref[start : start + count]
    held[len(refs) * count] = jnp.zeros_like(held[0])


def load_table(table, refs):
    at = 0
    for ref in refs:
        table[pl.ds(at, ref.shape[0]), :] = ref[...]
        at += ref.shape[0]


def for_pairs(pairs_ref, counts_ref, room, groups, base, block, body):
    for g in groups:

        @pl.loop(0, pl.cdiv(counts_ref[g], batch))
        def _(b):
            entries = []
            for q in range(batch):
                e = pairs_ref[g * room + b * batch + q]
                at = pl.multiple_of(((e & 255) - base) * block, block)
                entries.append((at, (e >> 8) & 15, (e >> 12) & 255, e >> 20))
            body(entries)


def first_kernel(cfg, pairs_ref, counts_ref, observed, *refs):
    sku_starts, piece_count, out_count, room, groups, base, block = cfg
    sku_count = len(sku_starts)
    skus = refs[:sku_count]
    pieces = refs[sku_count : sku_count + piece_count]
    outs = refs[-3 - out_count : -3]
    held, table, grad = refs[-3:]
    load_skus(held, skus, sku_starts)
    load_table(table, pieces)
    grad[...] = jnp.zeros_like(grad)

    def body(entries):
        terms = []
        for at, n, sku_at, slot in entries:
            sku = held[sku_at]
            predicted = lax.dot_general(
                table[pl.ds(at, block), :], sku, NT, preferred_element_type=jnp.float32
            )
            misfit = predicted - observed[slot, n].T.astype(jnp.float32)
            terms.append(
                jnp.dot(misfit.astype(jnp.bfloat16), sku, preferred_element_type=jnp.float32)
            )
        for (at, _, _, _), term in zip(entries, terms):
            grad[pl.ds(at, block), :] += term

    for_pairs(pairs_ref, counts_ref, room, groups, base, block, body)
    at = 0
    for out in outs:
        out[...] = grad[pl.ds(at, out.shape[0]), :].astype(jnp.bfloat16)
        at += out.shape[0]


def first_pass(pairs, counts, observed, skus, pieces, plan, groups, marks):
    offsets = [d for g in groups for d in plan.groups[g]]
    given = [piece for d in offsets for piece in pieces[d]]
    cuts = [plan.cuts(d) for d in offsets]
    heights = [b - a for spans in cuts for a, b in spans]
    skus, sku_starts = zip(*skus)
    block, rank = plan.block, skus[0].shape[2]
    room = pairs.shape[0] // len(plan.groups)
    slots = len(skus) * skus[0].shape[0]
    cfg = (sku_starts, len(given), len(heights), room, groups, plan.starts[groups[0]], block)
    table = (len(offsets) * plan.rows, rank)
    inputs = [observed, *skus, *given, *marks]
    out = pl.pallas_call(
        functools.partial(first_kernel, cfg),
        out_shape=[VMEM((height, rank), jnp.bfloat16) for height in heights],
        in_specs=[spec(SMEM)] * 2 + [spec(VMEM)] * len(inputs),
        out_specs=[spec(VMEM)] * len(heights),
        scratch_shapes=[
            VMEM((slots + 1, block, rank), jnp.bfloat16),
            VMEM(table, jnp.bfloat16),
            VMEM(table, jnp.float32),
        ],
        compiler_params=params(24),
        cost_estimate=cost(len(offsets) * room // plan.count, block, rank),
    )(pairs, counts, *map(near, inputs))
    out = list(out)
    return {d: [out.pop(0) for _ in spans] for d, spans in zip(offsets, cuts)}


def second_kernel(cfg, row_ref, live_ref, ids_ref, observed, *refs):
    ks, sku_starts, per_owner, kinds, block = cfg
    skus, pieces = refs[: len(ks)], refs[len(ks) : -1 - len(ks)]
    outs, table = refs[-1 - len(ks) : -1], refs[-1]
    load_table(table, pieces)
    row = row_ref[0]
    for k, sku_ref, start, out in zip(ks, skus, sku_starts, outs):
        out[...] = jnp.zeros_like(out)
        owner = row ^ k

        @pl.loop(0, live_ref[owner])
        def _(i):
            slot = owner * per_owner + i
            stores, measured = [], []
            for n in range(kinds):
                at = pl.multiple_of(ids_ref[n, slot] * block, block)
                stores.append(table[pl.ds(at, block), :])
                measured.append(observed[slot, n])
            store = jnp.concatenate(stores, axis=0)
            predicted = lax.dot_general(
                sku_ref[start + i], store, NT, preferred_element_type=jnp.float32
            )
            misfit = predicted - jnp.concatenate(measured, axis=1).astype(jnp.float32)
            out[i] = jnp.dot(
                misfit.astype(jnp.bfloat16), store, preferred_element_type=jnp.float32
            ).astype(jnp.bfloat16)


def second_pass(ks, row, live, ids, observed, skus, pieces, plan, per_owner):
    kept, sku_starts = zip(*[skus[k] for k in ks])
    kinds, block, rank = observed.shape[1], plan.block, kept[0].shape[2]
    shape = (per_owner, block, rank)
    inputs = [observed, *kept, *[piece for d in plan.order for piece in pieces[d]]]
    return pl.pallas_call(
        functools.partial(second_kernel, (ks, sku_starts, per_owner, kinds, block)),
        out_shape=[VMEM(shape, jnp.bfloat16)] * len(ks),
        in_specs=[spec(SMEM)] * 3 + [spec(VMEM)] * len(inputs),
        out_specs=[spec(VMEM)] * len(ks),
        scratch_shapes=[VMEM((plan.count * plan.rows, rank), jnp.bfloat16)],
        compiler_params=params(16),
        cost_estimate=cost(len(ks) * per_owner * kinds, block, rank),
    )(row, live, ids, *map(near, inputs))


def take_terms(held, ids, terms, row, per_owner):
    blocks = []
    for block_ids, term in zip(ids, terms):
        for i in range(per_owner):
            block = block_ids[row * per_owner + i]
            held[block] -= learn_rate * term[i].astype(jnp.float32)
            blocks.append(block)
    return blocks


def copy_out(held, out, blocks, sems):
    copies = [
        pltpu.make_async_copy(held.at[block], out.at[block], sems.at[n])
        for n, block in enumerate(blocks)
    ]
    for copy in copies:
        copy.start()
    for copy in copies:
        copy.wait()


def base_kernel(count, per_owner, row_ref, *refs):
    ids, sku, terms = refs[:count], refs[count], refs[count + 1 : -3]
    held, out, sems = refs[-3:]
    held[...] = sku[...] * (1.0 - learn_rate * weight_decay)
    take_terms(held, ids, terms, row_ref[0], per_owner)
    copy_out(held, out, range(sku.shape[0]), sems)


def base_step(row, ids, sku, terms, per_owner):
    return pl.pallas_call(
        functools.partial(base_kernel, len(ids), per_owner),
        out_shape=[VMEM(sku.shape, jnp.float32), pltpu.HBM(sku.shape, jnp.float32)],
        in_specs=[spec(SMEM)] * (len(ids) + 1) + [spec(VMEM)] * (1 + len(ids)),
        out_specs=[spec(VMEM), spec(pltpu.HBM)],
        scratch_shapes=[pltpu.SemaphoreType.DMA((sku.shape[0],))],
        compiler_params=params(8),
    )(row, *ids, sku, *map(near, terms))


def finish_kernel(count, per_owner, row_ref, *refs):
    ids, sku, terms = refs[:count], refs[count], refs[count + 1 : 2 * count + 1]
    out, held, sems = refs[-3:]
    for block_ids in ids:
        for i in range(per_owner):
            block = block_ids[row_ref[0] * per_owner + i]
            held[block] = sku[block]
    blocks = take_terms(held, ids, terms, row_ref[0], per_owner)
    copy_out(held, out, blocks, sems)


def finish_step(row, ids, held, out, terms, per_owner):
    return pl.pallas_call(
        functools.partial(finish_kernel, len(ids), per_owner),
        out_shape=pltpu.HBM(out.shape, jnp.float32),
        in_specs=[spec(SMEM)] * (len(ids) + 1)
        + [spec(VMEM)] * (1 + len(ids))
        + [spec(pltpu.HBM)],
        out_specs=spec(pltpu.HBM),
        scratch_shapes=[
            VMEM(out.shape, jnp.float32),
            pltpu.SemaphoreType.DMA((len(ids) * per_owner,)),
        ],
        input_output_aliases={2 + 2 * len(ids): 0},
        compiler_params=params(4),
    )(row, *ids, near(held), *map(near, terms), away(out))


def local(observed, sku_ids, store_ids, live_slot_counts, sku_factors, store_factors):
    row_count = lax.axis_size("row")
    per_owner = observed.shape[0] // row_count
    kinds, block = observed.shape[1:3]
    rank = sku_factors.shape[1]
    plan = Plan(lax.axis_size("col"), store_factors.shape[0], block)
    row_vec = lax.axis_index("row").reshape(1).astype(jnp.int32)
    live = live_slot_counts.reshape(row_count)
    sku = sku_factors.reshape(-1, block, rank)

    swaps = [[(r, r ^ k) for r in range(row_count)] for k in range(row_count)]
    asked = [sku_ids] + [lax.ppermute(sku_ids, "row", swaps[k]) for k in range(1, row_count)]
    place = ring_place(lax.axis_index("col"), plan.count)
    store_ids = store_ids.T
    owner_place = ring_place(store_ids // plan.blocks, plan.count)
    arrival = plan.arrival((owner_place - place) % plan.count)
    ids = arrival * plan.blocks + store_ids % plan.blocks
    pairs, counts, listed = list_pairs(
        row_vec, live, ids, plan, row_count, per_owner, kinds, rank
    )
    picked = pick(row_vec, asked, sku, per_owner, listed)
    pieces = gather_ring(store_factors.astype(jnp.bfloat16), plan)

    observed, is_held = hold(observed, pieces[1] + pieces[plan.count - 1])
    direct, through = [], []
    for x in range(1, row_count // 2):
        direct.append(lax.ppermute(picked[2 * x], "row", swaps[2 * x]))
        onward = after(after(picked[2 * x + 1], direct[-1][0]), is_held)
        through.append(lax.ppermute(onward, "row", swaps[2 * x]))
    late = pieces[plan.far - 1] + pieces[plan.far + 1]
    passed = lax.ppermute(join(picked[1], through, per_owner, late), "row", swaps[1])
    skus = [(picked[0], 0), (passed, 0)]
    for x, blocks in enumerate(direct, 1):
        skus += [(blocks, 0), (passed, x * per_owner)]

    grads, marks = {}, []
    for group in (2, 3, 1, 0):
        if plan.groups[group]:
            some = first_pass(pairs, counts, observed, skus, pieces, plan, [group], marks)
            grads.update(some)
            marks = some[plan.groups[group][0]][:1]
    own_grad = (scatter_split if split_sum else scatter_ring)(grads, plan)

    def step_of(grad):
        return store_factors - learn_rate * (grad + weight_decay * store_factors)

    new_low = step_of(own_grad).astype(jnp.bfloat16)
    new_pieces = (gather_split if split_gather else gather_ring)(new_low, plan)

    terms = [None] * row_count
    for ks in (list(range(2, row_count)), [1, 0]):
        out = second_pass(ks, row_vec, live, ids, observed, skus, new_pieces, plan, per_owner)
        for k, term in zip(ks, out):
            terms[k] = lax.ppermute(term, "row", swaps[k]) if k else term
    held, new_sku = base_step(row_vec, asked[:2], sku, terms[:2], per_owner)
    new_sku = finish_step(row_vec, asked[2:], held, new_sku, terms[2:], per_owner)
    new_store = step_of(after(own_grad, new_pieces[plan.far][1]))
    return new_sku.reshape(sku_factors.shape), new_store


def solution(mesh):
    placed = (
        P(("row", "col"), None, None, None),
        P(("row", "col")),
        P(("row", "col"), None),
        P("row", "col", None),
        P(("row", "col"), None),
        P(("row", "col"), None),
    )
    return jax.shard_map(
        local,
        mesh=mesh,
        in_specs=placed,
        out_specs=(P(("row", "col"), None), P(("row", "col"), None)),
        check_vma=False,
    )
```

```python
import functools

import jax
import jax.numpy as jnp
from jax import lax
from jax.experimental import pallas as pl
from jax.experimental.pallas import tpu as pltpu
from jax.sharding import PartitionSpec as P

learn_rate = 0.01
weight_decay = 0.05
line_len = 4
batch = 8
split_sum = False
split_gather = True

VMEM = pltpu.VMEM
SMEM = pltpu.SMEM
NT = (((1,), (1,)), ((), ()))


def spec(space):
    return pl.BlockSpec(memory_space=space)


def near(array):
    return pltpu.with_memory_space_constraint(array, VMEM)


def away(array):
    return pltpu.with_memory_space_constraint(array, pltpu.HBM)


def params(mib):
    return pltpu.CompilerParams(vmem_limit_bytes=mib * 1024 * 1024)


def cost(pairs, block, rank):
    return pl.CostEstimate(
        flops=pairs * 4 * block * block * rank,
        bytes_accessed=pairs * 256 * 1024,
        transcendentals=0,
    )


def ring_place(col, col_count):
    width = max(col_count // line_len, 1)
    depth = col_count // width
    across, along = col % width, col // width
    return across * depth + jnp.where(across % 2 == 0, along, depth - 1 - along)


def ring_steps(col_count):
    width = max(col_count // line_len, 1)
    depth = col_count // width
    order = []
    for place in range(col_count):
        across, along = divmod(place, depth)
        along = along if across % 2 == 0 else depth - 1 - along
        order.append(along * width + across)
    ahead = [(order[p], order[(p + 1) % col_count]) for p in range(col_count)]
    back = [(b, a) for a, b in ahead]
    return ahead, back


class Plan:
    def __init__(self, col_count, rows, block):
        self.count = col_count
        self.far = col_count // 2
        self.rows, self.block = rows, block
        self.blocks = rows // block
        first = (self.blocks + 1) // 2 * block
        self.halves = [(0, first), (first, rows)]
        self.order = [0]
        for m in range(1, self.far):
            self.order += [m, col_count - m]
        self.order.append(self.far)
        self.groups = [self.order[:3], self.order[3:-3], self.order[-3:-1], self.order[-1:]]
        self.starts = [self.order.index(g[0]) * self.blocks for g in self.groups]

    def arrival(self, offset):
        back = self.count - offset
        return jnp.where(
            offset == 0,
            0,
            jnp.where(
                offset == self.far,
                self.count - 1,
                jnp.where(offset < self.far, 2 * offset - 1, 2 * back),
            ),
        )

    def cuts(self, offset):
        return self.halves if split_sum or offset == self.far else [(0, self.rows)]


def after(value, mark):
    return jnp.where(mark[:1] < jnp.inf, value, jnp.zeros_like(value))


def gather_ring(low, plan, marks=None, arrived=None):
    steps = ring_steps(plan.count)
    moved = [low, low]
    pieces = {0: [low]}
    for step in range(1, plan.far + 1):
        if step == plan.far:
            moved = [moved[way][a:b] for way, (a, b) in enumerate(plan.halves)]
        if marks is not None and step in marks:
            moved = [after(value, marks[step]) for value in moved]
        moved = [lax.ppermute(moved[way], "col", steps[way]) for way in (0, 1)]
        if step == plan.far:
            pieces[step] = moved
        else:
            pieces[plan.count - step] = moved[:1]
            pieces[step] = moved[1:]
        if arrived:
            arrived(step, pieces)
    return pieces


def gather_split(low, plan):
    steps = ring_steps(plan.count)
    parts = [low[a:b] for a, b in plan.halves]
    moved = {(way, h): parts[h] for way in (0, 1) for h in (0, 1)}
    pieces = {offset: [None, None] for offset in plan.order}
    pieces[0] = parts
    for step in range(1, plan.far + 1):
        for h in (0, 1):
            for way in (0, 1):
                if step < plan.far or way == h:
                    moved[way, h] = lax.ppermute(moved[way, h], "col", steps[way])
                    pieces[step if way else plan.count - step][h] = moved[way, h]
    return pieces


def add_up(moved, piece):
    return (moved.astype(jnp.float32) + piece.astype(jnp.float32)).astype(jnp.bfloat16)


def scatter_ring(pieces, plan):
    steps = ring_steps(plan.count)
    first = plan.halves[0][1]
    moved = [lax.ppermute(pieces[plan.far][way], "col", steps[way]) for way in (0, 1)]
    for step in range(plan.far - 1, 0, -1):
        for way in (0, 1):
            (value,) = pieces[plan.count - step if way else step]
            if step == plan.far - 1:
                parts = [value[:first], value[first:]]
                parts[way] = add_up(moved[way], parts[way])
                value = jnp.concatenate(parts, axis=0)
            else:
                value = add_up(moved[way], value)
            moved[way] = lax.ppermute(value, "col", steps[way])
    return (
        pieces[0][0].astype(jnp.float32)
        + moved[0].astype(jnp.float32)
        + moved[1].astype(jnp.float32)
    )


def scatter_split(pieces, plan):
    steps = ring_steps(plan.count)
    moved = {}
    for step in range(plan.far, 0, -1):
        for h in (0, 1):
            for way in (0, 1):
                if step < plan.far or way == h:
                    value = pieces[plan.count - step if way else step][h]
                    if (way, h) in moved:
                        value = add_up(moved[way, h], value)
                    moved[way, h] = lax.ppermute(value, "col", steps[way])
    return jnp.concatenate(
        [
            pieces[0][h].astype(jnp.float32)
            + moved[0, h].astype(jnp.float32)
            + moved[1, h].astype(jnp.float32)
            for h in (0, 1)
        ],
        axis=0,
    )


def pick_kernel(row_count, per_owner, row_ref, *refs):
    ids = refs[:row_count]
    table, _, *outs = refs[row_count:-2]
    held, sems = refs[-2:]
    row = row_ref[0]

    def block_of(k, i):
        n = k * per_owner + i
        block = ids[k][row * per_owner + i]
        return pltpu.make_async_copy(table.at[block], held.at[n], sems.at[n])

    order = [(k, i) for k in reversed(range(row_count)) for i in range(per_owner)]
    for k, i in order:
        block_of(k, i).start()
    for k, i in order:
        block_of(k, i).wait()
        outs[k][i] = held[k * per_owner + i].astype(jnp.bfloat16)


def pick(row, ids, table, per_owner, mark):
    row_count = len(ids)
    block, rank = table.shape[1:]
    shapes = [VMEM((per_owner, block, rank), jnp.bfloat16)] * row_count
    asked = row_count * per_owner
    return pl.pallas_call(
        functools.partial(pick_kernel, row_count, per_owner),
        out_shape=shapes,
        in_specs=[spec(SMEM)] * (row_count + 1) + [spec(pltpu.HBM), spec(VMEM)],
        out_specs=[spec(VMEM)] * len(shapes),
        scratch_shapes=[
            VMEM((asked, block, rank), jnp.float32),
            pltpu.SemaphoreType.DMA((asked,)),
        ],
        compiler_params=params(8),
    )(row, *ids, away(table), near(mark))


def join_kernel(per_owner, first, *refs):
    out = refs[-1]
    out[0:per_owner] = first[...]
    for x in range(1, out.shape[0] // per_owner):
        out[x * per_owner : (x + 1) * per_owner] = refs[x - 1][...]


def join(first, moved, per_owner, marks):
    shape = ((1 + len(moved)) * per_owner,) + first.shape[1:]
    inputs = [first, *moved, *marks]
    return pl.pallas_call(
        functools.partial(join_kernel, per_owner),
        out_shape=VMEM(shape, first.dtype),
        in_specs=[spec(VMEM)] * len(inputs),
        out_specs=spec(VMEM),
        compiler_params=params(1),
    )(*map(near, inputs))


def list_kernel(cfg, row_ref, live_ref, ids_ref, pairs_ref, counts_ref, mark):
    row_count, per_owner, kinds, starts, room = cfg
    mark[...] = jnp.zeros_like(mark)
    row = row_ref[0]
    counts = (jnp.int32(0),) * len(starts)
    for owner in range(row_count):

        def add_slot(i, counts):
            slot = owner * per_owner + i
            sku_at = (row ^ owner) * per_owner + i
            tag = sku_at * 4096 + slot * 1048576
            for n in range(kinds):
                at = ids_ref[n, slot]
                group, filled = jnp.int32(0), counts[0]
                for g, start in enumerate(starts[1:], 1):
                    group = jnp.where(at >= start, g, group)
                    filled = jnp.where(at >= start, counts[g], filled)
                pairs_ref[group * room + filled] = at + n * 256 + tag
                counts = tuple(
                    count + (group == g).astype(jnp.int32) for g, count in enumerate(counts)
                )
            return counts

        counts = lax.fori_loop(0, live_ref[owner], add_slot, counts)

    for g, count in enumerate(counts):
        counts_ref[g] = count
    for g, start in enumerate(starts):
        for q in range(batch - 1):
            blank = start + row_count * per_owner * 4096
            pairs_ref[g * room + counts[g] + q] = jnp.int32(blank)


def list_pairs(row, live, ids, plan, row_count, per_owner, kinds, rank):
    room = row_count * per_owner * kinds + batch
    groups = len(plan.groups)
    return pl.pallas_call(
        functools.partial(list_kernel, (row_count, per_owner, kinds, plan.starts, room)),
        out_shape=[
            jax.ShapeDtypeStruct((groups * room,), jnp.int32),
            jax.ShapeDtypeStruct((groups,), jnp.int32),
            VMEM((8, rank), jnp.float32),
        ],
        in_specs=[spec(SMEM)] * 3,
        out_specs=[spec(SMEM)] * 2 + [spec(VMEM)],
        compiler_params=params(1),
    )(row, live, ids)


def hold_kernel(observed, *refs):
    held, mark, sems = refs[-3:]
    copies = [
        pltpu.make_async_copy(observed.at[slot], held.at[slot], sems.at[slot])
        for slot in range(observed.shape[0])
    ]
    for copy in copies:
        copy.start()
    mark[...] = jnp.zeros_like(mark)
    for copy in copies:
        copy.wait()


def hold(observed, marks):
    return pl.pallas_call(
        hold_kernel,
        out_shape=[
            VMEM(observed.shape, observed.dtype),
            VMEM((8, marks[0].shape[1]), jnp.float32),
        ],
        in_specs=[spec(pltpu.HBM)] + [spec(VMEM)] * len(marks),
        out_specs=[spec(VMEM)] * 2,
        scratch_shapes=[pltpu.SemaphoreType.DMA((observed.shape[0],))],
        compiler_params=params(1),
    )(away(observed), *map(near, marks))


def load_skus(held, refs, starts):
    count = refs[0].shape[0]
    for k, (ref, start) in enumerate(zip(refs, starts)):
        held[pl.ds(k * count, count)] = ref[start : start + count]
    held[len(refs) * count] = jnp.zeros_like(held[0])


def load_table(table, refs):
    at = 0
    for ref in refs:
        table[pl.ds(at, ref.shape[0]), :] = ref[...]
        at += ref.shape[0]


def for_pairs(pairs_ref, counts_ref, room, groups, base, block, body):
    for g in groups:

        @pl.loop(0, pl.cdiv(counts_ref[g], batch))
        def _(b):
            entries = []
            for q in range(batch):
                e = pairs_ref[g * room + b * batch + q]
                at = pl.multiple_of(((e & 255) - base) * block, block)
                entries.append((at, (e >> 8) & 15, (e >> 12) & 255, e >> 20))
            body(entries)


def first_kernel(cfg, pairs_ref, counts_ref, observed, *refs):
    sku_starts, piece_count, out_count, room, groups, base, block = cfg
    sku_count = len(sku_starts)
    skus = refs[:sku_count]
    pieces = refs[sku_count : sku_count + piece_count]
    outs = refs[-3 - out_count : -3]
    held, table, grad = refs[-3:]
    load_skus(held, skus, sku_starts)
    load_table(table, pieces)
    grad[...] = jnp.zeros_like(grad)

    def body(entries):
        terms = []
        for at, n, sku_at, slot in entries:
            sku = held[sku_at]
            predicted = lax.dot_general(
                table[pl.ds(at, block), :], sku, NT, preferred_element_type=jnp.float32
            )
            misfit = predicted - observed[slot, n].T.astype(jnp.float32)
            terms.append(
                jnp.dot(misfit.astype(jnp.bfloat16), sku, preferred_element_type=jnp.float32)
            )
        for (at, _, _, _), term in zip(entries, terms):
            grad[pl.ds(at, block), :] += term

    for_pairs(pairs_ref, counts_ref, room, groups, base, block, body)
    at = 0
    for out in outs:
        out[...] = grad[pl.ds(at, out.shape[0]), :].astype(jnp.bfloat16)
        at += out.shape[0]


def first_pass(pairs, counts, observed, skus, pieces, plan, groups, marks):
    offsets = [d for g in groups for d in plan.groups[g]]
    given = [piece for d in offsets for piece in pieces[d]]
    cuts = [plan.cuts(d) for d in offsets]
    heights = [b - a for spans in cuts for a, b in spans]
    skus, sku_starts = zip(*skus)
    block, rank = plan.block, skus[0].shape[2]
    room = pairs.shape[0] // len(plan.groups)
    slots = len(skus) * skus[0].shape[0]
    cfg = (sku_starts, len(given), len(heights), room, groups, plan.starts[groups[0]], block)
    table = (len(offsets) * plan.rows, rank)
    inputs = [observed, *skus, *given, *marks]
    out = pl.pallas_call(
        functools.partial(first_kernel, cfg),
        out_shape=[VMEM((height, rank), jnp.bfloat16) for height in heights],
        in_specs=[spec(SMEM)] * 2 + [spec(VMEM)] * len(inputs),
        out_specs=[spec(VMEM)] * len(heights),
        scratch_shapes=[
            VMEM((slots + 1, block, rank), jnp.bfloat16),
            VMEM(table, jnp.bfloat16),
            VMEM(table, jnp.float32),
        ],
        compiler_params=params(24),
        cost_estimate=cost(len(offsets) * room // plan.count, block, rank),
    )(pairs, counts, *map(near, inputs))
    out = list(out)
    return {d: [out.pop(0) for _ in spans] for d, spans in zip(offsets, cuts)}


def second_kernel(cfg, row_ref, live_ref, ids_ref, observed, *refs):
    ks, sku_starts, piece_count, per_owner, kinds, block = cfg
    skus, pieces = refs[: len(ks)], refs[len(ks) : len(ks) + piece_count]
    if piece_count > 1:
        *outs, table = refs[-1 - len(ks) :]
        load_table(table, pieces)
    else:
        outs, (table,) = refs[-len(ks) :], pieces
    row = row_ref[0]
    for k, sku_ref, start, out in zip(ks, skus, sku_starts, outs):
        out[...] = jnp.zeros_like(out)
        owner = row ^ k

        @pl.loop(0, live_ref[owner])
        def _(i):
            slot = owner * per_owner + i
            stores, measured = [], []
            for n in range(kinds):
                at = pl.multiple_of(ids_ref[n, slot] * block, block)
                stores.append(table[pl.ds(at, block), :])
                measured.append(observed[slot, n])
            store = jnp.concatenate(stores, axis=0)
            predicted = lax.dot_general(
                sku_ref[start + i], store, NT, preferred_element_type=jnp.float32
            )
            misfit = predicted - jnp.concatenate(measured, axis=1).astype(jnp.float32)
            out[i] = jnp.dot(
                misfit.astype(jnp.bfloat16), store, preferred_element_type=jnp.float32
            ).astype(jnp.bfloat16)


def second_pass(ks, row, live, ids, observed, skus, pieces, plan, per_owner, marks):
    kept, sku_starts = zip(*[skus[k] for k in ks])
    kinds, block, rank = observed.shape[1], plan.block, kept[0].shape[2]
    shape = (per_owner, block, rank)
    given = [pieces]
    out_shape = [VMEM(shape, jnp.bfloat16)] * len(ks)
    if isinstance(pieces, dict):
        given = [piece for d in plan.order for piece in pieces[d]]
        out_shape.append(VMEM((plan.count * plan.rows, rank), jnp.bfloat16))
    inputs = [observed, *kept, *given, *marks]
    return pl.pallas_call(
        functools.partial(second_kernel, (ks, sku_starts, len(given), per_owner, kinds, block)),
        out_shape=out_shape,
        in_specs=[spec(SMEM)] * 3 + [spec(VMEM)] * len(inputs),
        out_specs=[spec(VMEM)] * len(out_shape),
        compiler_params=params(8),
        cost_estimate=cost(len(ks) * per_owner * kinds, block, rank),
    )(row, live, ids, *map(near, inputs))


def take_terms(held, ids, terms, row, per_owner):
    blocks = []
    for block_ids, term in zip(ids, terms):
        for i in range(per_owner):
            block = block_ids[row * per_owner + i]
            held[block] -= learn_rate * term[i].astype(jnp.float32)
            blocks.append(block)
    return blocks


def copy_out(held, out, blocks, sems):
    copies = [
        pltpu.make_async_copy(held.at[block], out.at[block], sems.at[n])
        for n, block in enumerate(blocks)
    ]
    for copy in copies:
        copy.start()
    for copy in copies:
        copy.wait()


def base_kernel(count, per_owner, row_ref, *refs):
    ids, sku, terms = refs[:count], refs[count], refs[count + 1 : -3]
    held, out, sems = refs[-3:]
    held[...] = sku[...] * (1.0 - learn_rate * weight_decay)
    take_terms(held, ids, terms, row_ref[0], per_owner)
    copy_out(held, out, range(sku.shape[0]), sems)


def base_step(row, ids, sku, terms, per_owner):
    return pl.pallas_call(
        functools.partial(base_kernel, len(ids), per_owner),
        out_shape=[VMEM(sku.shape, jnp.float32), pltpu.HBM(sku.shape, jnp.float32)],
        in_specs=[spec(SMEM)] * (len(ids) + 1) + [spec(VMEM)] * (1 + len(ids)),
        out_specs=[spec(VMEM), spec(pltpu.HBM)],
        scratch_shapes=[pltpu.SemaphoreType.DMA((sku.shape[0],))],
        compiler_params=params(8),
    )(row, *ids, sku, *map(near, terms))


def finish_kernel(per_owner, row_ref, ids, term, *refs):
    held, out, sems = refs[-3:]
    blocks = take_terms(held, [ids], [term], row_ref[0], per_owner)
    copy_out(held, out, blocks, sems)


def finish_step(row, ids, held, out, term, per_owner):
    return pl.pallas_call(
        functools.partial(finish_kernel, per_owner),
        out_shape=[VMEM(held.shape, jnp.float32), pltpu.HBM(out.shape, jnp.float32)],
        in_specs=[spec(SMEM)] * 2 + [spec(VMEM)] * 2 + [spec(pltpu.HBM)],
        out_specs=[spec(VMEM), spec(pltpu.HBM)],
        scratch_shapes=[pltpu.SemaphoreType.DMA((per_owner,))],
        input_output_aliases={3: 0, 4: 1},
        compiler_params=params(1),
    )(row, ids, near(term), near(held), away(out))


def local(observed, sku_ids, store_ids, live_slot_counts, sku_factors, store_factors):
    row_count = lax.axis_size("row")
    per_owner = observed.shape[0] // row_count
    kinds, block = observed.shape[1:3]
    rank = sku_factors.shape[1]
    plan = Plan(lax.axis_size("col"), store_factors.shape[0], block)
    row_vec = lax.axis_index("row").reshape(1).astype(jnp.int32)
    live = live_slot_counts.reshape(row_count)
    sku = sku_factors.reshape(-1, block, rank)

    swaps = [[(r, r ^ k) for r in range(row_count)] for k in range(row_count)]
    asked = [sku_ids] + [lax.ppermute(sku_ids, "row", swaps[k]) for k in range(1, row_count)]
    place = ring_place(lax.axis_index("col"), plan.count)
    store_ids = store_ids.T
    owner_place = ring_place(store_ids // plan.blocks, plan.count)
    arrival = plan.arrival((owner_place - place) % plan.count)
    ids = arrival * plan.blocks + store_ids % plan.blocks
    pairs, counts, listed = list_pairs(
        row_vec, live, ids, plan, row_count, per_owner, kinds, rank
    )
    picked = pick(row_vec, asked, sku, per_owner, listed)
    pieces = gather_ring(store_factors.astype(jnp.bfloat16), plan)

    observed, is_held = hold(observed, pieces[1] + pieces[plan.count - 1])
    direct, through = [], []
    for x in range(1, row_count // 2):
        direct.append(lax.ppermute(picked[2 * x], "row", swaps[2 * x]))
        onward = after(after(picked[2 * x + 1], direct[-1][0]), is_held)
        through.append(lax.ppermute(onward, "row", swaps[2 * x]))
    late = pieces[plan.far - 1] + pieces[plan.far + 1]
    passed = lax.ppermute(join(picked[1], through, per_owner, late), "row", swaps[1])
    skus = [(picked[0], 0), (passed, 0)]
    for x, blocks in enumerate(direct, 1):
        skus += [(blocks, 0), (passed, x * per_owner)]

    grads, marks = {}, []
    for group in (2, 3, 1, 0):
        if plan.groups[group]:
            some = first_pass(pairs, counts, observed, skus, pieces, plan, [group], marks)
            grads.update(some)
            marks = some[plan.groups[group][0]][:1]
    own_grad = (scatter_split if split_sum else scatter_ring)(grads, plan)

    def step_of(grad):
        return store_factors - learn_rate * (grad + weight_decay * store_factors)

    new_low = step_of(own_grad).astype(jnp.bfloat16)
    new_pieces = (gather_split if split_gather else gather_ring)(new_low, plan)

    terms, table, marks = [None] * row_count, new_pieces, []
    for ks in [[k] for k in range(row_count - 1, 1, -1)] + [[1, 0]]:
        out = second_pass(
            ks, row_vec, live, ids, observed, skus, table, plan, per_owner, marks
        )
        marks = out[:1]
        if len(out) > len(ks):
            table = out[-1]
        for k, term in zip(ks, out):
            terms[k] = lax.ppermute(term, "row", swaps[k]) if k else term
    held, new_sku = base_step(row_vec, asked[:2], sku, terms[:2], per_owner)
    for k in range(row_count - 1, 1, -1):
        held, new_sku = finish_step(row_vec, asked[k], held, new_sku, terms[k], per_owner)
    new_store = step_of(after(own_grad, new_pieces[plan.far][1]))
    return new_sku.reshape(sku_factors.shape), new_store


def solution(mesh):
    placed = (
        P(("row", "col"), None, None, None),
        P(("row", "col")),
        P(("row", "col"), None),
        P("row", "col", None),
        P(("row", "col"), None),
        P(("row", "col"), None),
    )
    return jax.shard_map(
        local,
        mesh=mesh,
        in_specs=placed,
        out_specs=(P(("row", "col"), None), P(("row", "col"), None)),
        check_vma=False,
    )
```
